256 devices in a mesh: row: 16 (over y_lo, x, core), blk: 16 (over z, y_hi).
Axes of the slice: x: 4, y: 4 (y_hi: 2, y_lo: 2; y = y_hi * 2 + y_lo), z: 8, core: 2. Of those that a mesh axis runs over, the one named last changes fastest.
Arguments:
- values: bfloat16 [1024, 16, 256, 256], P('row', 'blk'), may hold values from -6 to 6
- scales: bfloat16 [1024, 16], P('row', 'blk'), may hold values from 0.0049743652 to 0.049804688
- pattern: int32 [1024, 16], P('row', 'blk'), may hold values from 0 to 2047, as said below
- omega: bfloat16 [2048, 256, 128], P(('row', 'blk')), may hold values from -6 to 6
Outputs:
- basis: float32 [2048, 256, 128], P(('row', 'blk'))
- upper: float32 [128, 128], replicated
The draws below stay inside these ranges and needn't reach their ends.
Inputs may be any that keep to these rules, and one draw needn't show every extreme that they name: `pattern`: A block-row of group g = r // 64 has all its column blocks in g * 128 to (g + 1) * 128 - 1. Among the 64 blocks of one device (its block-rows and its positions), at most 4 lie in one aligned run of 8 column blocks, and some run holds exactly 4.
All inputs are finite; a program needn't handle non-finite values.
Results may differ from the reference program's by a relative error of at most 0.0003.
Values may be sent and summed in bfloat16 or wider, within the bound.
No kernel may reach another device: no remote copies, remote signals or barrier semaphores. Data moves between devices by JAX's collectives and lax.ppermute only.
A program may use at most 128 MiB of HBM per device.

```python
import math
import jax
import jax.numpy as jnp
from jax import lax

BS = 256
P_SIZE = 128
NCB = 2048
K = 16
RB = 64
KDEV = 1
MB = 1024
CAP = 4


def draw_pattern(key, part):
    block_count = RB * KDEV
    cycle_size = K // KDEV
    row_groups = MB // RB
    col_per_dev = NCB // (row_groups * cycle_size)

    def one_device(index):
        device_key = jax.random.fold_in(key, index)
        key_hot, key_perm, key_local = jax.random.split(device_key, 3)
        hot_owner = jax.random.randint(key_hot, (), 0, cycle_size)
        slots = jnp.arange(block_count)
        others = (hot_owner + 1 + (slots - CAP) % (cycle_size - 1)) % cycle_size
        owner_list = jnp.where(slots < CAP, hot_owner, others)
        owner_list = jax.random.permutation(key_perm, owner_list)
        local_list = jax.random.randint(key_local, (block_count,), 0, col_per_dev)
        group_base = index // cycle_size * col_per_dev * cycle_size
        return (group_base + owner_list * col_per_dev + local_list).reshape(RB, KDEV)
    tables = jax.vmap(one_device)(jnp.arange(row_groups * cycle_size))
    return tables.reshape(row_groups, cycle_size, RB, KDEV).transpose(0, 2, 1, 3).reshape(MB, K).astype(jnp.int32)


def levels(own_key, shape, cuts, smallest, largest):
    def one(dim, parts):
        steps = jax.random.uniform(jax.random.fold_in(jax.random.fold_in(own_key, 6), dim), (parts,), jnp.float32, smallest / len(cuts), largest / len(cuts))
        return jnp.repeat(jnp.exp(steps), shape[dim] // parts).reshape((-1,) + (1,) * (len(shape) - dim - 1))

    gain = one(*cuts[0])
    for cut in cuts[1:]:
        gain = gain * one(*cut)
    return gain


def normal_values(stream_key, shape, width, reach, pieces=(), dtype=jnp.bfloat16):
    result = width * jax.random.normal(stream_key, shape, jnp.float32)
    if pieces:
        result = result * levels(stream_key, shape, pieces, -0.22, 0.18)
    return jnp.clip(result, -reach, reach).astype(dtype)


def setup_inputs(seed: int = 0) -> dict:
    key_of = jax.random.split(jax.random.key(seed), 5)
    return {
        "values": normal_values(key_of[0], (MB, K, BS, BS), 1.0, 6.0, ((0, 16), (1, 16))),
        "scales": jnp.clip(jnp.exp(math.log(0.049804688) - 2.3038113 * jax.random.uniform(key_of[1], (MB, K), jnp.float32) ** levels(key_of[1], (MB, K), ((0, 16), (1, 16)), -0.2, 0.2)), 0.0049743652, 0.049804688).astype(jnp.bfloat16),
        "pattern": draw_pattern(jax.random.fold_in(key_of[4], 71), 0),
        "omega": normal_values(key_of[3], (NCB, BS, P_SIZE), 1.0, 6.0, ((0, 256),)),
    }


def reference(values, scales, pattern, omega):
    weights = scales.astype(jnp.float32)

    def row_product(item_tuple):
        blocks, scale_row, col_blocks = item_tuple
        picked = jnp.take(omega, col_blocks, axis=0).astype(jnp.float32)
        products = jnp.einsum('kij,kjc->kic', blocks.astype(jnp.float32), picked) * scale_row[:, None, None]
        partial_value = jnp.sum(products.reshape(K // KDEV, KDEV, BS, P_SIZE), axis=1)
        return jnp.sum(partial_value, axis=0)
    rowvec = lax.map(row_product, (values, weights, pattern))

    def add_row(running_sum, item_tuple):
        blocks, scale_row, col_blocks, row_vecs = item_tuple
        row_high = lax.optimization_barrier(row_vecs.astype(jnp.bfloat16))
        row_low = (row_vecs - row_high.astype(jnp.float32)).astype(jnp.bfloat16)
        blocks_wide = blocks.astype(jnp.float32)
        high_part = jnp.einsum('kji,jc->kic', blocks_wide, row_high.astype(jnp.float32))
        low_part = jnp.einsum('kji,jc->kic', blocks_wide, row_low.astype(jnp.float32))
        contrib = (high_part + low_part) * scale_row[:, None, None]
        return (running_sum.at[col_blocks].add(contrib), None)
    start_sum = jnp.zeros((NCB, BS, P_SIZE), jnp.float32)
    colsum, unused = lax.scan(add_row, start_sum, (values, weights, pattern, rowvec))
    flat_sum = colsum.reshape(NCB * BS, P_SIZE)
    gram = jnp.dot(flat_sum.T, flat_sum, precision=lax.Precision.HIGHEST) / (NCB * BS)
    lower_factor = jnp.linalg.cholesky(gram)
    solved = jax.scipy.linalg.solve_triangular(lower_factor, flat_sum.T, lower=True)
    return (solved.T.reshape(NCB, BS, P_SIZE), lower_factor.T)
```

```python
import functools

import jax
import jax.numpy as jnp
from jax import lax
from jax.experimental import pallas as pl
from jax.experimental.pallas import tpu as pltpu
from jax.sharding import PartitionSpec as P

BS = 256
NCB = 2048
META = 16
TOP = 32700.0
VMEM = 56 * 1024 * 1024


def put_coded(ref, index, x, extra):
    rows = x.shape[0]
    top = jnp.max(jnp.abs(x), axis=0, keepdims=True)
    expo = jnp.clip(jnp.ceil(jnp.log2(jnp.maximum(top, 1e-30))), -90.0, 120.0)
    frac = jnp.minimum(jnp.ceil(top * jnp.exp2(-expo) * 256.0 + 0.5), 300.0)
    inverse = TOP * 256.0 * jnp.exp2(-expo) / frac
    ref[index, pl.ds(0, rows)] = jnp.round(x * inverse).astype(jnp.int32).astype(jnp.int16)
    place = lax.broadcasted_iota(jnp.int32, (META, x.shape[1]), 0)
    meta = jnp.where(place == 0, expo.astype(jnp.int32), frac.astype(jnp.int32))
    meta = jnp.where(place == 2, extra, meta)
    ref[index, pl.ds(rows, META)] = meta.astype(jnp.int16)


def scale_of(meta):
    meta = meta.astype(jnp.int32).astype(jnp.float32)
    return jnp.exp2(meta[0:1]) * meta[1:2] * (1.0 / (256.0 * TOP))


def z_shift(size, step):
    half = size // 2
    return [(z * 2 + y, (z + step) % half * 2 + y) for z in range(half) for y in range(2)]


def ring(own, size):
    length = size // 2
    reach = length // 2
    ahead, back = z_shift(size, 1), z_shift(size, -1)
    rows = own.shape[0]
    pieces = [(0, 0, own)]
    up, down = own, own
    for step in range(1, reach):
        up = lax.ppermute(up, "blk", ahead)
        down = lax.ppermute(down, "blk", back)
        pieces += [(-step, 0, up), (step, 0, down)]
    pieces.append((-reach, 0, lax.ppermute(up[: rows // 2], "blk", ahead)))
    pieces.append((reach, rows // 2, lax.ppermute(down[rows // 2 :], "blk", back)))
    return pieces


def gather_pieces(x):
    size = lax.axis_size("blk")
    me = lax.axis_index("blk")
    z, y = me // 2, me % 2
    swapped = lax.ppermute(x, "blk", [(b, b ^ 1) for b in range(size)])
    arrays, starts = [], []
    for flip, own in ((0, x), (1, swapped)):
        for offset, first, piece in ring(own, size):
            owner = (z + offset + size) % (size // 2) * 2 + (y + flip) % 2
            arrays.append(piece)
            starts.append(owner * x.shape[0] + first)
    return arrays, jnp.stack(starts).astype(jnp.int32)


def fetch_pieces(starts, pieces, slab, sems):
    copies = [
        pltpu.make_async_copy(
            piece, slab.at[pl.ds(starts[i], piece.shape[0])], sems.at[i]
        )
        for i, piece in enumerate(pieces)
    ]
    for copy in copies:
        copy.start()
    for copy in copies:
        copy.wait()


STEP = 4


def product_kernel(count, cols, starts, scales, values_ref, *refs):
    pieces, out_ref, slab, sems = refs[:count], refs[count], refs[count + 1], refs[count + 2]
    step = pl.program_id(0)

    @pl.when(step == 0)
    def _():
        fetch_pieces(starts, pieces, slab, sems)

    for i in range(STEP):
        at = step * STEP + i
        product = jnp.dot(values_ref[i], slab[cols[at]], preferred_element_type=jnp.float32)
        put_coded(out_ref, i, product * scales[at], 0)


def products(values, cols, scales, pieces, starts):
    blocks, side, width = values.shape[0], values.shape[1], pieces[0].shape[2]
    total = sum(p.shape[0] for p in pieces)
    return pl.pallas_call(
        functools.partial(product_kernel, len(pieces)),
        out_shape=jax.ShapeDtypeStruct((blocks, side + META, width), jnp.int16),
        grid_spec=pltpu.PrefetchScalarGridSpec(
            num_scalar_prefetch=3,
            grid=(blocks // STEP,),
            in_specs=[pl.BlockSpec((STEP, side, side), lambda s, *_: (s, 0, 0))]
            + [pl.BlockSpec(memory_space=pl.ANY)] * len(pieces),
            out_specs=pl.BlockSpec((STEP, side + META, width), lambda s, *_: (s, 0, 0)),
            scratch_shapes=[
                pltpu.VMEM((total, side, width), pieces[0].dtype),
                pltpu.SemaphoreType.DMA((len(pieces),)),
            ],
        ),
        compiler_params=pltpu.CompilerParams(vmem_limit_bytes=VMEM),
    )(cols, starts, scales, values, *pieces)


def row_sum_kernel(in_ref, out_ref):
    sources, _, tall, width = in_ref.shape
    rows = tall - META
    total = jnp.zeros((rows, width), jnp.float32)
    for i in range(sources):
        scale = scale_of(in_ref[i, 0, pl.ds(rows, META)])
        total += in_ref[i, 0, pl.ds(0, rows)].astype(jnp.int32).astype(jnp.float32) * scale
    put_coded(out_ref, 0, total, 0)


def row_sums(parts):
    sources, rows, tall, width = parts.shape
    return pl.pallas_call(
        row_sum_kernel,
        out_shape=jax.ShapeDtypeStruct((rows, tall, width), jnp.int16),
        grid=(rows,),
        in_specs=[pl.BlockSpec((sources, 1, tall, width), lambda r: (0, r, 0, 0))],
        out_specs=pl.BlockSpec((1, tall, width), lambda r: (r, 0, 0)),
        compiler_params=pltpu.CompilerParams(vmem_limit_bytes=VMEM),
    )(parts)


def contrib_kernel(count, order, slots, scales, starts, *refs):
    blocks = refs[:STEP]
    pieces = refs[STEP : STEP + count]
    out_ref, slab, sems = refs[STEP + count :]
    step = pl.program_id(0)

    @pl.when(step == 0)
    def _():
        fetch_pieces(starts, pieces, slab, sems)

    for i in range(STEP):
        at = step * STEP + i
        row = order[at]
        side = blocks[i].shape[1]
        code = slab[row, pl.ds(0, side)].astype(jnp.int32).astype(jnp.float32)
        high = code.astype(jnp.bfloat16)
        low = (code - high.astype(jnp.float32)).astype(jnp.bfloat16)
        both = jnp.concatenate([high, low], axis=1)
        product = lax.dot_general(
            blocks[i][0], both, (((0,), (0,)), ((), ())), preferred_element_type=jnp.float32
        )
        width = high.shape[1]
        weight = scale_of(slab[row, pl.ds(side, META)]) * scales[row]
        put_coded(out_ref, i, (product[:, :width] + product[:, width:]) * weight, slots[at])


def contribs(values, order, slots, scales, pieces, starts):
    blocks, side = values.shape[:2]
    tall, width = pieces[0].shape[1:]
    total = sum(p.shape[0] for p in pieces)

    def block_at(i):
        return pl.BlockSpec((1, side, side), lambda s, order, *_: (order[s * STEP + i], 0, 0))

    return pl.pallas_call(
        functools.partial(contrib_kernel, len(pieces)),
        out_shape=jax.ShapeDtypeStruct((blocks, tall, width), jnp.int16),
        grid_spec=pltpu.PrefetchScalarGridSpec(
            num_scalar_prefetch=4,
            grid=(blocks // STEP,),
            in_specs=[block_at(i) for i in range(STEP)]
            + [pl.BlockSpec(memory_space=pl.ANY)] * len(pieces),
            out_specs=pl.BlockSpec((STEP, tall, width), lambda s, *_: (s, 0, 0)),
            scratch_shapes=[
                pltpu.VMEM((total, tall, width), pieces[0].dtype),
                pltpu.SemaphoreType.DMA((len(pieces),)),
            ],
        ),
        compiler_params=pltpu.CompilerParams(vmem_limit_bytes=VMEM),
    )(order, slots, scales, starts, *([values] * STEP), *pieces)


def column_kernel(slots, in_ref, out_ref, gram_ref):
    step = pl.program_id(0)
    count, tall, width = in_ref.shape
    rows = tall - META

    @pl.when(step == 0)
    def _():
        out_ref[...] = jnp.zeros_like(out_ref)

    for i in range(count):
        slot = slots[step * count + i]
        scale = scale_of(in_ref[i, pl.ds(rows, META)])
        out_ref[slot] += in_ref[i, pl.ds(0, rows)].astype(jnp.int32).astype(jnp.float32) * scale

    @pl.when(step == pl.num_programs(0) - 1)
    def _():
        gram_ref[...] = jnp.zeros_like(gram_ref)
        for c in range(out_ref.shape[0]):
            block = out_ref[c]
            gram_ref[...] += lax.dot_general(
                block,
                block,
                (((0,), (0,)), ((), ())),
                precision=lax.Precision.HIGHEST,
                preferred_element_type=jnp.float32,
            )


def column_sums(parts, slots, columns):
    blocks, tall, width = parts.shape
    batch = 8
    return pl.pallas_call(
        column_kernel,
        out_shape=(
            jax.ShapeDtypeStruct((columns, tall - META, width), jnp.float32),
            jax.ShapeDtypeStruct((width, width), jnp.float32),
        ),
        grid_spec=pltpu.PrefetchScalarGridSpec(
            num_scalar_prefetch=1,
            grid=(blocks // batch,),
            in_specs=[pl.BlockSpec((batch, tall, width), lambda s, *_: (s, 0, 0))],
            out_specs=(
                pl.BlockSpec((columns, tall - META, width), lambda s, *_: (0, 0, 0)),
                pl.BlockSpec((width, width), lambda s, *_: (0, 0)),
            ),
        ),
        compiler_params=pltpu.CompilerParams(vmem_limit_bytes=VMEM),
    )(slots, parts)


def gram_total(gram):
    size = gram.shape[0]
    parts = lax.axis_size("row")
    some = lax.all_to_all(gram, "row", 0, 0, tiled=True)
    some = jnp.sum(some.reshape(parts, size // parts, size), axis=0)
    count = lax.axis_size("blk")
    some = jnp.broadcast_to(some[None], (count,) + some.shape)
    some = jnp.sum(lax.all_to_all(some, "blk", 0, 0, tiled=True), axis=0)
    some = jnp.broadcast_to(some[None], (parts,) + some.shape)
    return lax.all_to_all(some, "row", 0, 0, tiled=True).reshape(size, size)


PANEL = 8


def factor_kernel(gram_ref, sums_ref, basis_ref, upper_ref, g_ref, m_ref):
    size = gram_ref.shape[0]
    across = lax.broadcasted_iota(jnp.int32, (PANEL, size), 1)
    down = lax.broadcasted_iota(jnp.int32, (PANEL, size), 0)
    g_ref[...] = gram_ref[...] * (1.0 / (NCB * BS))
    m_ref[...] = (
        lax.broadcasted_iota(jnp.int32, (size, size), 0)
        == lax.broadcasted_iota(jnp.int32, (size, size), 1)
    ).astype(jnp.float32)
    for first in range(0, size, PANEL):
        panel = g_ref[pl.ds(first, PANEL), :]
        other = m_ref[pl.ds(first, PANEL), :]
        for k in range(PANEL):
            j = first + k
            column = panel[:, j : j + 1]
            pivot = column[k : k + 1]
            inverse = lax.rsqrt(pivot)
            inverse = inverse * (1.5 - 0.5 * pivot * inverse * inverse)
            row = panel[k : k + 1] * inverse
            other_row = other[k : k + 1] * inverse
            column = column * inverse
            below = down > k
            panel = jnp.where(below, panel - column * row, jnp.where(down == k, row, panel))
            other = jnp.where(
                below, other - column * other_row, jnp.where(down == k, other_row, other)
            )
        panel = jnp.where(across >= down + first, panel, 0.0)
        upper_ref[pl.ds(first, PANEL), :] = panel
        m_ref[pl.ds(first, PANEL), :] = other
        rest = size - first - PANEL
        if rest:
            both = jnp.concatenate([panel, other], axis=1)
            update = lax.dot_general(
                panel,
                both,
                (((0,), (0,)), ((), ())),
                precision=lax.Precision.HIGHEST,
                preferred_element_type=jnp.float32,
            )
            g_ref[pl.ds(first + PANEL, rest), :] -= update[first + PANEL :, :size]
            m_ref[pl.ds(first + PANEL, rest), :] -= update[first + PANEL :, size:]
    for c in range(sums_ref.shape[0]):
        basis_ref[c] = lax.dot_general(
            sums_ref[c],
            m_ref[...],
            (((1,), (1,)), ((), ())),
            precision=lax.Precision.HIGHEST,
            preferred_element_type=jnp.float32,
        )


def factor(gram, sums):
    return pl.pallas_call(
        factor_kernel,
        out_shape=(
            jax.ShapeDtypeStruct(sums.shape, jnp.float32),
            jax.ShapeDtypeStruct(gram.shape, jnp.float32),
        ),
        in_specs=[pl.BlockSpec(memory_space=pltpu.VMEM)] * 2,
        out_specs=(pl.BlockSpec(memory_space=pltpu.VMEM),) * 2,
        scratch_shapes=[pltpu.VMEM(gram.shape, jnp.float32)] * 2,
        compiler_params=pltpu.CompilerParams(vmem_limit_bytes=VMEM),
    )(gram, sums)


def local(values, scales, pattern, omega):
    blocks = pattern.size
    columns, side, width = omega.shape
    parts = lax.axis_size("blk")
    tall = side + META
    values = values.reshape(blocks, side, side)
    cols = pattern.reshape(-1) - lax.axis_index("row") * columns * parts
    weights = scales.astype(jnp.float32).reshape(-1)
    key = cols * blocks + lax.iota(jnp.int32, blocks)
    rank = jnp.sum((key[None, :] < key[:, None]).astype(jnp.int32), axis=1)
    chosen = rank[None, :] == lax.iota(jnp.int32, blocks)[:, None]
    order = jnp.sum(jnp.where(chosen, lax.iota(jnp.int32, blocks)[None, :], 0), axis=1)
    slots = jnp.sum(jnp.where(chosen, cols[None, :], 0), axis=1) % columns

    pieces, starts = gather_pieces(omega)
    coded = products(values, cols, weights, pieces, starts)
    coded = lax.all_to_all(coded, "blk", 0, 0, tiled=True)
    rowvec = row_sums(coded.reshape(parts, blocks // parts, tall, width))
    pieces, starts = gather_pieces(rowvec)
    coded = contribs(values, order, slots, weights, pieces, starts)
    coded = lax.all_to_all(coded, "blk", 0, 0, tiled=True)
    sums, gram = column_sums(coded, coded[:, side + 2, 0].astype(jnp.int32), columns)
    return factor(gram_total(gram), sums)


def solution(mesh):
    return jax.shard_map(
        local,
        mesh=mesh,
        in_specs=(
            P("row", "blk", None, None),
            P("row", "blk"),
            P("row", "blk"),
            P(("row", "blk"), None, None),
        ),
        out_specs=(P(("row", "blk"), None, None), P()),
        check_vma=False,
    )
```

```python
import functools

import jax
import jax.numpy as jnp
from jax import lax
from jax.experimental import pallas as pl
from jax.experimental.pallas import tpu as pltpu
from jax.sharding import PartitionSpec as P

BS = 256
NCB = 2048
META = 16
TOP = 32700.0
VMEM = 56 * 1024 * 1024


def put_coded(ref, base, blocks, extras):
    rows, width = blocks[0].shape
    tops = [jnp.max(jnp.abs(x), axis=0, keepdims=True) for x in blocks]
    top = jnp.concatenate(tops, axis=0)
    expo = jnp.clip(jnp.ceil(jnp.log2(jnp.maximum(top, 1e-30))), -90.0, 120.0)
    small = jnp.exp2(-expo)
    frac = jnp.minimum(jnp.ceil(top * small * 256.0 + 0.5), 300.0)
    inverse = TOP * 256.0 * small / frac
    place = lax.broadcasted_iota(jnp.int32, (META, width), 0)
    for i, x in enumerate(blocks):
        code = jnp.round(x * inverse[i : i + 1]).astype(jnp.int32)
        ref[base + i, pl.ds(0, rows)] = code.astype(jnp.int16)
        meta = jnp.where(
            place == 0, expo[i : i + 1].astype(jnp.int32), frac[i : i + 1].astype(jnp.int32)
        )
        meta = jnp.where(place == 2, extras[i], meta)
        ref[base + i, pl.ds(rows, META)] = meta.astype(jnp.int16)


def scale_of(meta):
    meta = meta.astype(jnp.int32).astype(jnp.float32)
    return jnp.exp2(meta[0:1]) * meta[1:2] * (1.0 / (256.0 * TOP))


def decoded(ref, index):
    rows = ref.shape[1] - META
    code = ref[index, pl.ds(0, rows)].astype(jnp.int32).astype(jnp.float32)
    return code * scale_of(ref[index, pl.ds(rows, META)])


def cost(size):
    return pl.CostEstimate(flops=0, bytes_accessed=size, transcendentals=0)


STAGES = (
    ((0, 0), (-1, 0), (1, 0)),
    ((0, 1), (-1, 1), (1, 1), (-2, 0), (2, 0)),
    ((-2, 1), (2, 1), (-3, 0), (3, 0)),
    ((-3, 1), (3, 1), (4, 0)),
    ((4, 1),),
)


def z_shift(size, step):
    half = size // 2
    return [(z * 2 + y, (z + step) % half * 2 + y) for z in range(half) for y in range(2)]


def y_swap(x):
    return lax.ppermute(x, "blk", [(b, b ^ 1) for b in range(lax.axis_size("blk"))])


def up(x):
    return lax.ppermute(x, "blk", z_shift(lax.axis_size("blk"), 1))


def down(x):
    return lax.ppermute(x, "blk", z_shift(lax.axis_size("blk"), -1))


def owner_at(offset, flip):
    half = lax.axis_size("blk") // 2
    me = lax.axis_index("blk")
    return (me // 2 + offset + half) % half * 2 + (me % 2 + flip) % 2


def owner_table():
    return jnp.stack([owner_at(*o) for stage in STAGES for o in stage]).astype(jnp.int32)


def ring(own):
    half = own.shape[0] // 2
    found = {0: [(0, own)]}
    ahead, back = own, own
    for step in (1, 2, 3):
        ahead, back = up(ahead), down(back)
        found[-step], found[step] = [(0, ahead)], [(0, back)]
    found[4] = [(0, up(ahead[:half])), (half, down(back[half:]))]
    return found


def gather_shards(x, early):
    rows = x.shape[0]
    mine, other = ring(x), ring(y_swap(x[:early]))
    shards = {}
    for offset, parts in mine.items():
        shards[offset, 0] = [(a, 0, first, a.shape[0]) for first, a in parts]
    for offset, parts in other.items():
        shards[offset, 1] = [(a, 0, first, a.shape[0]) for first, a in parts]
    late = rows - early
    if late:
        for group in ((0, -1, 1), (-2, 2), (-3, 3, 4)):
            tails = [mine[o][-1][1][-late:] for o in group]
            swapped = y_swap(jnp.concatenate(tails))
            for i, o in enumerate(group):
                shards[o, 1].append((swapped, i * late, early, late))
    return shards


def stage_pieces(shards, stage, rows):
    arrays, moves = [], []
    for k, owner in enumerate(stage):
        for array, source, first, count in shards[owner]:
            at = [i for i, a in enumerate(arrays) if a is array]
            if not at:
                at = [len(arrays)]
                arrays.append(array)
            moves.append((at[0], source, k * rows + first, count))
    return arrays, moves


def start_moves(moves, pieces, slab, sems):
    copies = [
        pltpu.make_async_copy(
            pieces[a].at[pl.ds(source, count)], slab.at[pl.ds(target, count)], sems.at[i]
        )
        for i, (a, source, target, count) in enumerate(moves)
    ]
    for copy in copies:
        copy.start()
    return copies


def product_kernel(moves, arrays, base, owned, columns, *refs):
    owners, order, cols, weights, values = refs[:5]
    pieces = refs[5 : 5 + arrays]
    out, slab, blocks, results, slab_sems, block_sems, out_sems = refs[-7:]
    arrive = start_moves(moves, pieces, slab, slab_sems)
    which, loads = [], []
    for k in range(blocks.shape[0]):
        at = order[owners[base + k // owned] * owned + k % owned]
        which.append(at)
        loads.append(pltpu.make_async_copy(values.at[at], blocks.at[k], block_sems.at[k]))
        loads[-1].start()
    for copy in arrive:
        copy.wait()
    stores = []
    for k, at in enumerate(which):
        place = k // owned * columns + lax.rem(cols[at], columns)
        loads[k].wait()
        product = jnp.dot(blocks[k], slab[place], preferred_element_type=jnp.float32)
        results[k] = product * weights[at]
        stores.append(pltpu.make_async_copy(results.at[k], out.at[at], out_sems.at[k]))
        stores[-1].start()
    for copy in stores:
        copy.wait()


def products(values, order, cols, weights, shards, columns):
    blocks, side = values.shape[:2]
    owned = blocks // lax.axis_size("blk")
    owners = owner_table()
    result, base = None, 0
    for stage in STAGES:
        arrays, moves = stage_pieces(shards, stage, columns)
        width, count = arrays[0].shape[2], len(stage) * owned
        smem, hbm = pl.BlockSpec(memory_space=pltpu.SMEM), pl.BlockSpec(memory_space=pl.ANY)
        operands = [owners, order, cols, weights, values, *arrays]
        aliases = {}
        if result is not None:
            aliases = {len(operands): 0}
            operands.append(result)
        result = pl.pallas_call(
            functools.partial(product_kernel, moves, len(arrays), base, owned, columns),
            out_shape=jax.ShapeDtypeStruct((blocks, side, width), jnp.float32),
            in_specs=[smem] * 4 + [hbm] * (len(operands) - 4),
            out_specs=hbm,
            scratch_shapes=[
                pltpu.VMEM((len(stage) * columns, side, width), arrays[0].dtype),
                pltpu.VMEM((count, side, side), values.dtype),
                pltpu.VMEM((count, side, width), jnp.float32),
                pltpu.SemaphoreType.DMA((len(moves),)),
                pltpu.SemaphoreType.DMA((count,)),
                pltpu.SemaphoreType.DMA((count,)),
            ],
            input_output_aliases=aliases,
            compiler_params=pltpu.CompilerParams(vmem_limit_bytes=VMEM),
            cost_estimate=cost(count << 20),
        )(*operands)
        base += len(stage)
    return result


def combine_kernel(count, modes, place, products_ref, *refs):
    out_ref = refs[-1]
    for low in range(0, count, 4):
        blocks = []
        for i in range(low, low + 4):
            row = place[1] + i
            block = products_ref[0, row]
            for ref, mode in zip(refs, modes):
                if mode == "whole":
                    block += decoded(ref, row)
                elif mode == "first" and i < 4 or mode == "same":
                    block += decoded(ref, i)
                elif mode == "last" and i >= 4:
                    block += decoded(ref, i - 4)
            blocks.append(block)
        put_coded(out_ref, low, blocks, [0] * 4)


def combine(products_, chunk, row, count, *terms):
    tall, width = products_.shape[2] + META, products_.shape[3]
    place = jnp.stack([jnp.asarray(chunk, jnp.int32), jnp.asarray(row, jnp.int32)])
    arrays = [array for array, _ in terms]
    return pl.pallas_call(
        functools.partial(combine_kernel, count, [mode for _, mode in terms]),
        out_shape=jax.ShapeDtypeStruct((count, tall, width), jnp.int16),
        grid_spec=pltpu.PrefetchScalarGridSpec(
            num_scalar_prefetch=1,
            grid=(1,),
            in_specs=[pl.BlockSpec((1,) + products_.shape[1:], lambda s, p: (p[0], 0, 0, 0))]
            + [pl.BlockSpec(a.shape, lambda s, p: (0, 0, 0)) for a in arrays],
            out_specs=pl.BlockSpec((count, tall, width), lambda s, p: (0, 0, 0)),
        ),
        compiler_params=pltpu.CompilerParams(vmem_limit_bytes=VMEM),
        cost_estimate=cost(8 << 20),
    )(place, products_, *arrays)


def row_sums(product):
    half = lax.axis_size("blk") // 2
    me = lax.axis_index("blk")
    z, y = me // 2, me % 2
    product = product.reshape((half, product.shape[0] // half) + product.shape[1:])
    rows = product.shape[1]
    part = rows // 2

    def chunk(offset):
        return (z + offset + half) % half

    a = up(combine(product, chunk(4), 0, part))
    b = down(combine(product, chunk(4), part, part))
    a = up(combine(product, chunk(3), 0, rows, (a, "first")))
    b = down(combine(product, chunk(-3), 0, rows, (b, "last")))
    for step in (2, 1):
        a = up(combine(product, chunk(step), 0, rows, (a, "whole")))
        b = down(combine(product, chunk(-step), 0, rows, (b, "whole")))
    other = combine(product, z, (1 - y) * part, part, (a, "whole"), (b, "whole"))
    other = y_swap(other)
    return combine(product, z, y * part, part, (a, "whole"), (b, "whole"), (other, "same"))


def contrib_kernel(moves, arrays, base, owned, columns, *refs):
    owners, rank, cols, weights, values = refs[:5]
    pieces = refs[5 : 5 + arrays]
    out, slab, blocks, results, slab_sems, block_sems, out_sems = refs[-7:]
    arrive = start_moves(moves, pieces, slab, slab_sems)
    firsts, loads = [], []
    for k in range(blocks.shape[0] // owned):
        firsts.append(owners[base + k] * owned)
        loads.append(
            pltpu.make_async_copy(
                values.at[pl.ds(firsts[k], owned)],
                blocks.at[pl.ds(k * owned, owned)],
                block_sems.at[k],
            )
        )
        loads[-1].start()
    for copy in arrive:
        copy.wait()
    stores = []
    for k, first in enumerate(firsts):
        loads[k].wait()
        found = []
        for i in range(k * owned, (k + 1) * owned):
            at = first + i - k * owned
            side = blocks.shape[1]
            code = slab[i, pl.ds(0, side)].astype(jnp.int32).astype(jnp.float32)
            high = code.astype(jnp.bfloat16)
            low = (code - high.astype(jnp.float32)).astype(jnp.bfloat16)
            both = jnp.concatenate([high, low], axis=1)
            product = lax.dot_general(
                blocks[i], both, (((0,), (0,)), ((), ())), preferred_element_type=jnp.float32
            )
            width = high.shape[1]
            weight = scale_of(slab[i, pl.ds(side, META)]) * weights[at]
            found.append((product[:, :width] + product[:, width:]) * weight)
        extras = [lax.rem(cols[first + i], columns) for i in range(owned)]
        put_coded(results, k * owned, found, extras)
        for i in range(owned):
            slot = k * owned + i
            stores.append(
                pltpu.make_async_copy(
                    results.at[slot], out.at[rank[first + i]], out_sems.at[slot]
                )
            )
            stores[-1].start()
    for copy in stores:
        copy.wait()


def contribs(values, rank, cols, weights, shards, columns):
    blocks, side = values.shape[:2]
    owned = blocks // lax.axis_size("blk")
    owners = owner_table()
    result, base = None, 0
    for stage in STAGES:
        arrays, moves = stage_pieces(shards, stage, owned)
        tall, width = arrays[0].shape[1:]
        count = len(stage) * owned
        smem, hbm = pl.BlockSpec(memory_space=pltpu.SMEM), pl.BlockSpec(memory_space=pl.ANY)
        operands = [owners, rank, cols, weights, values, *arrays]
        aliases = {}
        if result is not None:
            aliases = {len(operands): 0}
            operands.append(result)
        result = pl.pallas_call(
            functools.partial(contrib_kernel, moves, len(arrays), base, owned, columns),
            out_shape=jax.ShapeDtypeStruct((blocks, tall, width), jnp.int16),
            in_specs=[smem] * 4 + [hbm] * (len(operands) - 4),
            out_specs=hbm,
            scratch_shapes=[
                pltpu.VMEM((count, tall, width), jnp.int16),
                pltpu.VMEM((count, side, side), values.dtype),
                pltpu.VMEM((count, tall, width), jnp.int16),
                pltpu.SemaphoreType.DMA((len(moves),)),
                pltpu.SemaphoreType.DMA((len(stage),)),
                pltpu.SemaphoreType.DMA((count,)),
            ],
            input_output_aliases=aliases,
            compiler_params=pltpu.CompilerParams(vmem_limit_bytes=VMEM),
            cost_estimate=cost(count << 20),
        )(*operands)
        base += len(stage)
    return result


def column_kernel(slots, in_ref, out_ref, gram_ref):
    step = pl.program_id(0)
    count = in_ref.shape[0]

    @pl.when(step == 0)
    def _():
        out_ref[...] = jnp.zeros_like(out_ref)

    for i in range(count):
        slot = slots[step * count + i]
        out_ref[slot] += decoded(in_ref, i)

    @pl.when(step == pl.num_programs(0) - 1)
    def _():
        gram_ref[...] = jnp.zeros_like(gram_ref)
        for c in range(out_ref.shape[0]):
            block = out_ref[c]
            gram_ref[...] += lax.dot_general(
                block,
                block,
                (((0,), (0,)), ((), ())),
                precision=lax.Precision.HIGHEST,
                preferred_element_type=jnp.float32,
            )


def column_sums(parts, slots, columns):
    blocks, tall, width = parts.shape
    batch = 8
    return pl.pallas_call(
        column_kernel,
        out_shape=(
            jax.ShapeDtypeStruct((columns, tall - META, width), jnp.float32),
            jax.ShapeDtypeStruct((width, width), jnp.float32),
        ),
        grid_spec=pltpu.PrefetchScalarGridSpec(
            num_scalar_prefetch=1,
            grid=(blocks // batch,),
            in_specs=[pl.BlockSpec((batch, tall, width), lambda s, *_: (s, 0, 0))],
            out_specs=(
                pl.BlockSpec((columns, tall - META, width), lambda s, *_: (0, 0, 0)),
                pl.BlockSpec((width, width), lambda s, *_: (0, 0)),
            ),
        ),
        compiler_params=pltpu.CompilerParams(vmem_limit_bytes=VMEM),
    )(slots, parts)


def gram_total(gram):
    size = gram.shape[0]
    parts = lax.axis_size("row")
    some = lax.all_to_all(gram, "row", 0, 0, tiled=True)
    some = jnp.sum(some.reshape(parts, size // parts, size), axis=0)
    count = lax.axis_size("blk")
    some = jnp.broadcast_to(some[None], (count,) + some.shape)
    some = jnp.sum(lax.all_to_all(some, "blk", 0, 0, tiled=True), axis=0)
    some = jnp.broadcast_to(some[None], (parts,) + some.shape)
    return lax.all_to_all(some, "row", 0, 0, tiled=True).reshape(size, size)


PANEL = 8


def factor_kernel(gram_ref, sums_ref, basis_ref, upper_ref, g_ref, m_ref):
    size = gram_ref.shape[0]
    across = lax.broadcasted_iota(jnp.int32, (PANEL, size), 1)
    down = lax.broadcasted_iota(jnp.int32, (PANEL, size), 0)
    g_ref[...] = gram_ref[...] * (1.0 / (NCB * BS))
    m_ref[...] = (
        lax.broadcasted_iota(jnp.int32, (size, size), 0)
        == lax.broadcasted_iota(jnp.int32, (size, size), 1)
    ).astype(jnp.float32)
    for first in range(0, size, PANEL):
        panel = g_ref[pl.ds(first, PANEL), :]
        other = m_ref[pl.ds(first, PANEL), :]
        for k in range(PANEL):
            j = first + k
            column = panel[:, j : j + 1]
            pivot = column[k : k + 1]
            inverse = lax.rsqrt(pivot)
            inverse = inverse * (1.5 - 0.5 * pivot * inverse * inverse)
            row = panel[k : k + 1] * inverse
            other_row = other[k : k + 1] * inverse
            column = column * inverse
            below = down > k
            panel = jnp.where(below, panel - column * row, jnp.where(down == k, row, panel))
            other = jnp.where(
                below, other - column * other_row, jnp.where(down == k, other_row, other)
            )
        panel = jnp.where(across >= down + first, panel, 0.0)
        upper_ref[pl.ds(first, PANEL), :] = panel
        m_ref[pl.ds(first, PANEL), :] = other
        rest = size - first - PANEL
        if rest:
            both = jnp.concatenate([panel, other], axis=1)
            update = lax.dot_general(
                panel,
                both,
                (((0,), (0,)), ((), ())),
                precision=lax.Precision.HIGHEST,
                preferred_element_type=jnp.float32,
            )
            g_ref[pl.ds(first + PANEL, rest), :] -= update[first + PANEL :, :size]
            m_ref[pl.ds(first + PANEL, rest), :] -= update[first + PANEL :, size:]
    for c in range(sums_ref.shape[0]):
        basis_ref[c] = lax.dot_general(
            sums_ref[c],
            m_ref[...],
            (((1,), (1,)), ((), ())),
            precision=lax.Precision.HIGHEST,
            preferred_element_type=jnp.float32,
        )


def factor(gram, sums):
    return pl.pallas_call(
        factor_kernel,
        out_shape=(
            jax.ShapeDtypeStruct(sums.shape, jnp.float32),
            jax.ShapeDtypeStruct(gram.shape, jnp.float32),
        ),
        in_specs=[pl.BlockSpec(memory_space=pltpu.VMEM)] * 2,
        out_specs=(pl.BlockSpec(memory_space=pltpu.VMEM),) * 2,
        scratch_shapes=[pltpu.VMEM(gram.shape, jnp.float32)] * 2,
        compiler_params=pltpu.CompilerParams(vmem_limit_bytes=VMEM),
    )(gram, sums)


def local(values, scales, pattern, omega):
    blocks = pattern.size
    columns, side, width = omega.shape
    parts = lax.axis_size("blk")
    values = values.reshape(blocks, side, side)
    cols = pattern.reshape(-1) - lax.axis_index("row") * columns * parts
    weights = scales.astype(jnp.float32).reshape(-1)
    count = lax.iota(jnp.int32, blocks)
    key = cols * blocks + count
    rank = jnp.sum((key[None, :] < key[:, None]).astype(jnp.int32), axis=1)
    order = jnp.sum(jnp.where(rank[None, :] == count[:, None], count[None, :], 0), axis=1)

    shards = gather_shards(omega, columns - columns // 4)
    product = products(values, order, cols, weights, shards, columns)
    rowvec = row_sums(product)
    shards = gather_shards(rowvec, rowvec.shape[0])
    coded = contribs(values, rank, cols, weights, shards, columns)
    coded = lax.all_to_all(coded, "blk", 0, 0, tiled=True)
    sums, gram = column_sums(coded, coded[:, side + 2, 0].astype(jnp.int32), columns)
    return factor(gram_total(gram), sums)


def solution(mesh):
    return jax.shard_map(
        local,
        mesh=mesh,
        in_specs=(
            P("row", "blk", None, None),
            P("row", "blk"),
            P("row", "blk"),
            P(("row", "blk"), None, None),
        ),
        out_specs=(P(("row", "blk"), None, None), P()),
        check_vma=False,
    )
```

```python
import functools

import jax
import jax.numpy as jnp
from jax import lax
from jax.experimental import pallas as pl
from jax.experimental.pallas import tpu as pltpu
from jax.sharding import PartitionSpec as P

BS = 256
NCB = 2048
META = 16
TOP = 32700.0
VMEM = 60 * 1024 * 1024


def put_coded(ref, base, blocks, extras):
    rows, width = blocks[0].shape
    tops = [jnp.max(jnp.abs(x), axis=0, keepdims=True) for x in blocks]
    top = jnp.concatenate(tops, axis=0)
    expo = jnp.clip(jnp.ceil(jnp.log2(jnp.maximum(top, 1e-30))), -90.0, 120.0)
    small = jnp.exp2(-expo)
    frac = jnp.minimum(jnp.ceil(top * small * 256.0 + 0.5), 300.0)
    inverse = TOP * 256.0 * small / frac
    place = lax.broadcasted_iota(jnp.int32, (META, width), 0)
    for i, x in enumerate(blocks):
        code = jnp.round(x * inverse[i : i + 1]).astype(jnp.int32)
        ref[base + i, pl.ds(0, rows)] = code.astype(jnp.int16)
        meta = jnp.where(
            place == 0, expo[i : i + 1].astype(jnp.int32), frac[i : i + 1].astype(jnp.int32)
        )
        meta = jnp.where(place == 2, extras[i], meta)
        ref[base + i, pl.ds(rows, META)] = meta.astype(jnp.int16)


def scale_of(meta):
    meta = meta.astype(jnp.int32).astype(jnp.float32)
    return jnp.exp2(meta[0:1]) * meta[1:2] * (1.0 / (256.0 * TOP))


def decoded(ref, index):
    rows = ref.shape[1] - META
    code = ref[index, pl.ds(0, rows)].astype(jnp.int32).astype(jnp.float32)
    return code * scale_of(ref[index, pl.ds(rows, META)])


def cost(size):
    return pl.CostEstimate(flops=0, bytes_accessed=size, transcendentals=0)


STAGES = (
    ((0, 0), (-1, 0), (1, 0)),
    ((0, 1), (-1, 1), (1, 1), (-2, 0), (2, 0)),
    ((-2, 1), (2, 1), (-3, 0), (3, 0)),
    ((-3, 1), (3, 1), (4, 0)),
    ((4, 1),),
)


def z_shift(size, step):
    half = size // 2
    return [(z * 2 + y, (z + step) % half * 2 + y) for z in range(half) for y in range(2)]


def y_swap(x):
    return lax.ppermute(x, "blk", [(b, b ^ 1) for b in range(lax.axis_size("blk"))])


def up(x):
    return lax.ppermute(x, "blk", z_shift(lax.axis_size("blk"), 1))


def down(x):
    return lax.ppermute(x, "blk", z_shift(lax.axis_size("blk"), -1))


def owner_at(offset, flip):
    half = lax.axis_size("blk") // 2
    me = lax.axis_index("blk")
    return (me // 2 + offset + half) % half * 2 + (me % 2 + flip) % 2


def owner_table():
    return jnp.stack([owner_at(*o) for stage in STAGES for o in stage]).astype(jnp.int32)


def gather_run(x, early, run):
    rows = x.shape[0]
    late = rows - early
    shards = {}

    def put(offset, flip, array, first=0):
        shards.setdefault((offset, flip), []).append((array, 0, first, array.shape[0]))

    def swap_tails(*offsets):
        if late:
            tails = [shards[o, 0][-1][0][-late:] for o in offsets]
            swapped = y_swap(jnp.concatenate(tails) if len(tails) > 1 else tails[0])
            for i, o in enumerate(offsets):
                shards.setdefault((o, 1), []).append((swapped, i * late, early, late))

    put(0, 0, x)
    other = y_swap(x[:early])
    put(0, 1, other)
    ahead, back = up(x), down(x)
    put(-1, 0, ahead)
    put(1, 0, back)
    swap_tails(0, -1, 1)
    ahead2, back2 = other, other
    result, base = None, 0
    for step in (1, 2, 3):
        if step < 3:
            ahead, back = up(ahead), down(back)
            put(-1 - step, 0, ahead)
            put(1 + step, 0, back)
        else:
            put(4, 0, up(ahead[: rows // 2]))
            put(4, 0, down(back[rows // 2 :]), rows // 2)
        ahead2, back2 = up(ahead2), down(back2)
        result = run(result, STAGES[step - 1], base, shards)
        base += len(STAGES[step - 1])
        ahead2, back2, result = lax.optimization_barrier((ahead2, back2, result))
        put(-step, 1, ahead2)
        put(step, 1, back2)
        swap_tails(*((-1 - step, 1 + step) if step < 3 else (4,)))
    put(4, 1, up(ahead2[: early // 2]))
    put(4, 1, down(back2[early // 2 :]), early // 2)
    for stage in STAGES[3:]:
        result = run(result, stage, base, shards)
        base += len(stage)
    return result


def stage_pieces(shards, stage, rows):
    arrays, moves = [], []
    for k, owner in enumerate(stage):
        for array, source, first, count in shards[owner]:
            at = [i for i, a in enumerate(arrays) if a is array]
            if not at:
                at = [len(arrays)]
                arrays.append(array)
            moves.append((at[0], source, k * rows + first, count))
    return arrays, moves


def start_moves(moves, pieces, slab, sems):
    copies = [
        pltpu.make_async_copy(
            pieces[a].at[pl.ds(source, count)], slab.at[pl.ds(target, count)], sems.at[i]
        )
        for i, (a, source, target, count) in enumerate(moves)
    ]
    for copy in copies:
        copy.start()
    return copies


def product_kernel(moves, arrays, base, owned, columns, *refs):
    owners, order, cols, weights, values = refs[:5]
    pieces = refs[5 : 5 + arrays]
    out, slab, blocks, results, slab_sems, block_sems, out_sems = refs[-7:]
    arrive = start_moves(moves, pieces, slab, slab_sems)
    which, loads = [], []
    for k in range(blocks.shape[0]):
        at = order[owners[base + k // owned] * owned + k % owned]
        which.append(at)
        loads.append(pltpu.make_async_copy(values.at[at], blocks.at[k], block_sems.at[k]))
        loads[-1].start()
    for copy in arrive:
        copy.wait()
    stores = []
    for k, at in enumerate(which):
        place = k // owned * columns + lax.rem(cols[at], columns)
        loads[k].wait()
        product = jnp.dot(blocks[k], slab[place], preferred_element_type=jnp.float32)
        results[k] = product * weights[at]
        stores.append(pltpu.make_async_copy(results.at[k], out.at[at], out_sems.at[k]))
        stores[-1].start()
    for copy in stores:
        copy.wait()


def products(values, order, cols, weights, shard, early, columns):
    blocks, side = values.shape[:2]
    owned = blocks // lax.axis_size("blk")
    owners = owner_table()

    def run(result, stage, base, shards):
        arrays, moves = stage_pieces(shards, stage, columns)
        width, count = arrays[0].shape[2], len(stage) * owned
        smem, hbm = pl.BlockSpec(memory_space=pltpu.SMEM), pl.BlockSpec(memory_space=pl.ANY)
        operands = [owners, order, cols, weights, values, *arrays]
        aliases = {}
        if result is not None:
            aliases = {len(operands): 0}
            operands.append(result)
        return pl.pallas_call(
            functools.partial(product_kernel, moves, len(arrays), base, owned, columns),
            out_shape=jax.ShapeDtypeStruct((blocks, side, width), jnp.float32),
            in_specs=[smem] * 4 + [hbm] * (len(operands) - 4),
            out_specs=hbm,
            scratch_shapes=[
                pltpu.VMEM((len(stage) * columns, side, width), arrays[0].dtype),
                pltpu.VMEM((count, side, side), values.dtype),
                pltpu.VMEM((count, side, width), jnp.float32),
                pltpu.SemaphoreType.DMA((len(moves),)),
                pltpu.SemaphoreType.DMA((count,)),
                pltpu.SemaphoreType.DMA((count,)),
            ],
            input_output_aliases=aliases,
            compiler_params=pltpu.CompilerParams(vmem_limit_bytes=VMEM),
            cost_estimate=cost(count << 20),
        )(*operands)

    return gather_run(shard, early, run)


def combine_kernel(count, modes, place, products_ref, *refs):
    out_ref = refs[-1]
    for low in range(0, count, 4):
        blocks = []
        for i in range(low, low + 4):
            row = place[1] + i
            block = products_ref[0, row]
            for ref, mode in zip(refs, modes):
                if mode == "whole":
                    block += decoded(ref, row)
                elif mode == "first" and i < 4 or mode == "same":
                    block += decoded(ref, i)
                elif mode == "last" and i >= 4:
                    block += decoded(ref, i - 4)
            blocks.append(block)
        put_coded(out_ref, low, blocks, [0] * 4)


def combine(products_, chunk, row, count, *terms):
    tall, width = products_.shape[2] + META, products_.shape[3]
    place = jnp.stack([jnp.asarray(chunk, jnp.int32), jnp.asarray(row, jnp.int32)])
    arrays = [array for array, _ in terms]
    return pl.pallas_call(
        functools.partial(combine_kernel, count, [mode for _, mode in terms]),
        out_shape=jax.ShapeDtypeStruct((count, tall, width), jnp.int16),
        grid_spec=pltpu.PrefetchScalarGridSpec(
            num_scalar_prefetch=1,
            grid=(1,),
            in_specs=[pl.BlockSpec((1,) + products_.shape[1:], lambda s, p: (p[0], 0, 0, 0))]
            + [pl.BlockSpec(a.shape, lambda s, p: (0, 0, 0)) for a in arrays],
            out_specs=pl.BlockSpec((count, tall, width), lambda s, p: (0, 0, 0)),
        ),
        compiler_params=pltpu.CompilerParams(vmem_limit_bytes=VMEM),
        cost_estimate=cost(8 << 20),
    )(place, products_, *arrays)


def row_sums(product):
    half = lax.axis_size("blk") // 2
    me = lax.axis_index("blk")
    z, y = me // 2, me % 2
    product = product.reshape((half, product.shape[0] // half) + product.shape[1:])
    rows = product.shape[1]
    part = rows // 2

    def chunk(offset):
        return (z + offset + half) % half

    a = up(combine(product, chunk(4), 0, part))
    b = down(combine(product, chunk(4), part, part))
    a = up(combine(product, chunk(3), 0, rows, (a, "first")))
    b = down(combine(product, chunk(-3), 0, rows, (b, "last")))
    for step in (2, 1):
        a = up(combine(product, chunk(step), 0, rows, (a, "whole")))
        b = down(combine(product, chunk(-step), 0, rows, (b, "whole")))
    other = combine(product, z, (1 - y) * part, part, (a, "whole"), (b, "whole"))
    other = y_swap(other)
    return combine(product, z, y * part, part, (a, "whole"), (b, "whole"), (other, "same"))


def contrib_kernel(moves, arrays, base, owned, columns, *refs):
    owners, rank, cols, weights, values = refs[:5]
    pieces = refs[5 : 5 + arrays]
    out, slab, blocks, results, slab_sems, block_sems, out_sems = refs[-7:]
    arrive = start_moves(moves, pieces, slab, slab_sems)
    firsts, loads = [], []
    for k in range(blocks.shape[0] // owned):
        firsts.append(owners[base + k] * owned)
        loads.append(
            pltpu.make_async_copy(
                values.at[pl.ds(firsts[k], owned)],
                blocks.at[pl.ds(k * owned, owned)],
                block_sems.at[k],
            )
        )
        loads[-1].start()
    for copy in arrive:
        copy.wait()
    stores = []
    for k, first in enumerate(firsts):
        loads[k].wait()
        found = []
        for i in range(k * owned, (k + 1) * owned):
            at = first + i - k * owned
            side = blocks.shape[1]
            code = slab[i, pl.ds(0, side)].astype(jnp.int32).astype(jnp.float32)
            high = code.astype(jnp.bfloat16)
            low = (code - high.astype(jnp.float32)).astype(jnp.bfloat16)
            both = jnp.concatenate([high, low], axis=1)
            product = lax.dot_general(
                blocks[i], both, (((0,), (0,)), ((), ())), preferred_element_type=jnp.float32
            )
            width = high.shape[1]
            weight = scale_of(slab[i, pl.ds(side, META)]) * weights[at]
            found.append((product[:, :width] + product[:, width:]) * weight)
        extras = [lax.rem(cols[first + i], columns) for i in range(owned)]
        put_coded(results, k * owned, found, extras)
        for i in range(owned):
            slot = k * owned + i
            stores.append(
                pltpu.make_async_copy(
                    results.at[slot], out.at[rank[first + i]], out_sems.at[slot]
                )
            )
            stores[-1].start()
    for copy in stores:
        copy.wait()


def contribs(values, rank, cols, weights, shard, early, columns):
    blocks, side = values.shape[:2]
    owned = blocks // lax.axis_size("blk")
    owners = owner_table()

    def run(result, stage, base, shards):
        arrays, moves = stage_pieces(shards, stage, owned)
        tall, width = arrays[0].shape[1:]
        count = len(stage) * owned
        smem, hbm = pl.BlockSpec(memory_space=pltpu.SMEM), pl.BlockSpec(memory_space=pl.ANY)
        operands = [owners, rank, cols, weights, values, *arrays]
        aliases = {}
        if result is not None:
            aliases = {len(operands): 0}
            operands.append(result)
        return pl.pallas_call(
            functools.partial(contrib_kernel, moves, len(arrays), base, owned, columns),
            out_shape=jax.ShapeDtypeStruct((blocks, tall, width), jnp.int16),
            in_specs=[smem] * 4 + [hbm] * (len(operands) - 4),
            out_specs=hbm,
            scratch_shapes=[
                pltpu.VMEM((count, tall, width), jnp.int16),
                pltpu.VMEM((count, side, side), values.dtype),
                pltpu.VMEM((count, tall, width), jnp.int16),
                pltpu.SemaphoreType.DMA((len(moves),)),
                pltpu.SemaphoreType.DMA((len(stage),)),
                pltpu.SemaphoreType.DMA((count,)),
            ],
            input_output_aliases=aliases,
            compiler_params=pltpu.CompilerParams(vmem_limit_bytes=VMEM),
            cost_estimate=cost(count << 20),
        )(*operands)

    return gather_run(shard, early, run)


def three_parts(x):
    high = x.astype(jnp.bfloat16)
    rest = x - high.astype(jnp.float32)
    middle = rest.astype(jnp.bfloat16)
    return high, middle, (rest - middle.astype(jnp.float32)).astype(jnp.bfloat16)


def dot_down(a, b):
    return lax.dot_general(a, b, (((0,), (0,)), ((), ())), preferred_element_type=jnp.float32)


def column_kernel(slots, in_ref, out_ref, gram_ref):
    step = pl.program_id(0)
    count = in_ref.shape[0]

    @pl.when(step == 0)
    def _():
        out_ref[...] = jnp.zeros_like(out_ref)

    for i in range(count):
        slot = slots[step * count + i]
        out_ref[slot] += decoded(in_ref, i)

    @pl.when(step == pl.num_programs(0) - 1)
    def _():
        width = gram_ref.shape[0]
        main = jnp.zeros((2 * width, 2 * width), jnp.float32)
        rest = jnp.zeros((width, width), jnp.float32)
        for c in range(out_ref.shape[0]):
            high, middle, low = three_parts(out_ref[c])
            pair = jnp.concatenate([high, middle], axis=1)
            main += dot_down(pair, pair)
            rest += dot_down(high, low)
        rest += main[:width, width:]
        gram_ref[...] = main[:width, :width] + (rest + rest.T + main[width:, width:])


def column_sums(parts, slots, columns):
    blocks, tall, width = parts.shape
    batch = 16
    return pl.pallas_call(
        column_kernel,
        out_shape=(
            jax.ShapeDtypeStruct((columns, tall - META, width), jnp.float32),
            jax.ShapeDtypeStruct((width, width), jnp.float32),
        ),
        grid_spec=pltpu.PrefetchScalarGridSpec(
            num_scalar_prefetch=1,
            grid=(blocks // batch,),
            in_specs=[pl.BlockSpec((batch, tall, width), lambda s, *_: (s, 0, 0))],
            out_specs=(
                pl.BlockSpec((columns, tall - META, width), lambda s, *_: (0, 0, 0)),
                pl.BlockSpec((width, width), lambda s, *_: (0, 0)),
            ),
        ),
        compiler_params=pltpu.CompilerParams(vmem_limit_bytes=VMEM),
    )(slots, parts)


def gram_total(gram):
    size = gram.shape[0]
    parts = lax.axis_size("row")
    some = lax.all_to_all(gram, "row", 0, 0, tiled=True)
    some = jnp.sum(some.reshape(parts, size // parts, size), axis=0)
    count = lax.axis_size("blk")
    some = jnp.broadcast_to(some[None], (count,) + some.shape)
    some = jnp.sum(lax.all_to_all(some, "blk", 0, 0, tiled=True), axis=0)
    some = jnp.broadcast_to(some[None], (parts,) + some.shape)
    return lax.all_to_all(some, "row", 0, 0, tiled=True).reshape(size, size)


PANEL = 32
GROUP = 4


def inverse_root(x):
    y = lax.rsqrt(x)
    return y * (1.5 - 0.5 * x * y * y)


def eliminate(panel, other, first, down):
    size = panel.shape[1]
    for q in range(0, PANEL, GROUP):
        j = first + q
        columns = [jnp.broadcast_to(panel[:, j + b : j + b + 1], panel.shape) for b in range(GROUP)]
        rows = [panel[q + a : q + a + 1] for a in range(GROUP)]
        others = [other[q + a : q + a + 1] for a in range(GROUP)]
        lower, inverse = {}, []
        for b in range(GROUP):
            for c in range(b, GROUP):
                entry = columns[c][q + b : q + b + 1]
                for k in range(b):
                    entry = entry - lower[b, k] * lower[c, k]
                if c == b:
                    inverse.append(inverse_root(entry))
                else:
                    lower[c, b] = entry * inverse[b]
        for b in range(GROUP):
            for k in range(b):
                rows[b] = rows[b] - lower[b, k] * rows[k]
                others[b] = others[b] - lower[b, k] * others[k]
                columns[b] = columns[b] - lower[b, k] * columns[k]
            rows[b] = rows[b] * inverse[b]
            others[b] = others[b] * inverse[b]
            columns[b] = columns[b] * inverse[b]
        if q + GROUP < PANEL:
            below = down >= q + GROUP
            change = sum(c * r for c, r in zip(columns, rows))
            panel = jnp.where(below, panel - change, panel)
            change = sum(c * r for c, r in zip(columns, others))
            other = jnp.where(below, other - change, other)
        for b in range(GROUP):
            panel = jnp.where(down == q + b, rows[b], panel)
            other = jnp.where(down == q + b, others[b], other)
    across = lax.broadcasted_iota(jnp.int32, (PANEL, size), 1)
    return jnp.where(across >= down + first, panel, 0.0), other


def factor_kernel(gram_ref, sums_ref, basis_ref, upper_ref, g_ref, m_ref):
    size = gram_ref.shape[0]
    down = lax.broadcasted_iota(jnp.int32, (PANEL, size), 0)
    g_ref[...] = gram_ref[...] * (1.0 / (NCB * BS))
    m_ref[...] = (
        lax.broadcasted_iota(jnp.int32, (size, size), 0)
        == lax.broadcasted_iota(jnp.int32, (size, size), 1)
    ).astype(jnp.float32)
    for first in range(0, size, PANEL):
        here, after = pl.ds(first, PANEL), pl.ds(first + PANEL, size - first - PANEL)
        panel, other = eliminate(g_ref[here, :], m_ref[here, :], first, down)
        upper_ref[here, :] = panel
        m_ref[here, :] = other
        if first + PANEL < size:
            high, middle, low = three_parts(panel)
            left = jnp.concatenate([high, middle, high, middle, high, low], axis=0)
            high, middle, low = three_parts(jnp.concatenate([panel, other], axis=1))
            right = jnp.concatenate([high, high, middle, middle, low, high], axis=0)
            update = dot_down(left, right)[first + PANEL :]
            g_ref[after, :] -= update[:, :size]
            m_ref[after, :] -= update[:, size:]
    high, middle, low = three_parts(m_ref[...].T)
    main = jnp.concatenate([jnp.concatenate([high, middle], axis=1)] * 2, axis=0)
    rest = jnp.concatenate([low, high], axis=0)
    for c in range(sums_ref.shape[0]):
        high, middle, low = three_parts(sums_ref[c])
        first = jnp.dot(
            jnp.concatenate([high, middle], axis=1), main, preferred_element_type=jnp.float32
        )
        second = jnp.dot(
            jnp.concatenate([high, low], axis=1), rest, preferred_element_type=jnp.float32
        )
        basis_ref[c] = first[:, :size] + (first[:, size:] + second)


def factor(gram, sums):
    return pl.pallas_call(
        factor_kernel,
        out_shape=(
            jax.ShapeDtypeStruct(sums.shape, jnp.float32),
            jax.ShapeDtypeStruct(gram.shape, jnp.float32),
        ),
        in_specs=[pl.BlockSpec(memory_space=pltpu.VMEM)] * 2,
        out_specs=(pl.BlockSpec(memory_space=pltpu.VMEM),) * 2,
        scratch_shapes=[pltpu.VMEM(gram.shape, jnp.float32)] * 2,
        compiler_params=pltpu.CompilerParams(vmem_limit_bytes=VMEM),
    )(gram, sums)


def local(values, scales, pattern, omega):
    blocks = pattern.size
    columns, side, width = omega.shape
    parts = lax.axis_size("blk")
    values = values.reshape(blocks, side, side)
    cols = pattern.reshape(-1) - lax.axis_index("row") * columns * parts
    weights = scales.astype(jnp.float32).reshape(-1)
    count = lax.iota(jnp.int32, blocks)
    key = cols * blocks + count
    rank = jnp.sum((key[None, :] < key[:, None]).astype(jnp.int32), axis=1)
    order = jnp.sum(jnp.where(rank[None, :] == count[:, None], count[None, :], 0), axis=1)

    product = products(values, order, cols, weights, omega, columns - columns // 4, columns)
    rowvec = row_sums(product)
    coded = contribs(values, rank, cols, weights, rowvec, rowvec.shape[0], columns)
    coded = lax.all_to_all(coded, "blk", 0, 0, tiled=True)
    sums, gram = column_sums(coded, coded[:, side + 2, 0].astype(jnp.int32), columns)
    return factor(gram_total(gram), sums)


def solution(mesh):
    return jax.shard_map(
        local,
        mesh=mesh,
        in_specs=(
            P("row", "blk", None, None),
            P("row", "blk"),
            P("row", "blk"),
            P(("row", "blk"), None, None),
        ),
        out_specs=(P(("row", "blk"), None, None), P()),
        check_vma=False,
    )
```

```python
import functools

import jax
import jax.numpy as jnp
from jax import lax
from jax.experimental import pallas as pl
from jax.experimental.pallas import tpu as pltpu
from jax.sharding import PartitionSpec as P

BS = 256
NCB = 2048
META = 16
TOP = 32700.0
QUAD = 4
VMEM = 60 * 1024 * 1024


def codes_of(blocks):
    tops = [jnp.max(jnp.abs(x), axis=0, keepdims=True) for x in blocks]
    top = jnp.concatenate(tops, axis=0)
    expo = jnp.clip(jnp.ceil(jnp.log2(jnp.maximum(top, 1e-30))), -90.0, 120.0)
    small = jnp.exp2(-expo)
    frac = jnp.minimum(jnp.ceil(top * small * 256.0 + 0.5), 300.0)
    inverse = TOP * 256.0 * small / frac
    codes = [
        jnp.round(x * inverse[i : i + 1]).astype(jnp.int32).astype(jnp.int16)
        for i, x in enumerate(blocks)
    ]
    return codes, expo.astype(jnp.int32), frac.astype(jnp.int32)


def put_coded(ref, base, blocks, extras):
    rows, width = blocks[0].shape
    codes, expo, frac = codes_of(blocks)
    place = lax.broadcasted_iota(jnp.int32, (META, width), 0)
    for i, code in enumerate(codes):
        ref[base + i, pl.ds(0, rows)] = code
        meta = jnp.where(place == 0, expo[i : i + 1], frac[i : i + 1])
        meta = jnp.where(place == 2, extras[i], meta)
        ref[base + i, pl.ds(rows, META)] = meta.astype(jnp.int16)


def put_quad(ref, index, blocks):
    rows, width = blocks[0].shape
    codes, expo, frac = codes_of(blocks)
    for i, code in enumerate(codes):
        ref[index, pl.ds(i * rows, rows)] = code
    spare = jnp.zeros((META - 2 * QUAD, width), jnp.int32)
    meta = jnp.concatenate([expo, frac, spare], axis=0)
    ref[index, pl.ds(QUAD * rows, META)] = meta.astype(jnp.int16)


def quad_scales(ref, index):
    meta = ref[index, pl.ds(ref.shape[1] - META, META)].astype(jnp.int32).astype(jnp.float32)
    return jnp.exp2(meta[:QUAD]) * meta[QUAD : 2 * QUAD] * (1.0 / (256.0 * TOP))


def quad_code(ref, index, i):
    rows = (ref.shape[1] - META) // QUAD
    return ref[index, pl.ds(i * rows, rows)].astype(jnp.int32).astype(jnp.float32)


def scale_of(meta):
    meta = meta.astype(jnp.int32).astype(jnp.float32)
    return jnp.exp2(meta[0:1]) * meta[1:2] * (1.0 / (256.0 * TOP))


def decoded(ref, index):
    rows = ref.shape[1] - META
    code = ref[index, pl.ds(0, rows)].astype(jnp.int32).astype(jnp.float32)
    return code * scale_of(ref[index, pl.ds(rows, META)])


def cost(size):
    return pl.CostEstimate(flops=0, bytes_accessed=size, transcendentals=0)


STAGES = (
    ((0, 0), (0, 1), (-1, 0), (1, 0)),
    ((-1, 1), (1, 1), (-2, 0), (-2, 1), (2, 0), (2, 1)),
    ((-3, 0), (-3, 1), (3, 0), (3, 1)),
    ((4, 0), (4, 1)),
)


def z_shift(size, step):
    half = size // 2
    return [(z * 2 + y, (z + step) % half * 2 + y) for z in range(half) for y in range(2)]


def y_swap(x):
    return lax.ppermute(x, "blk", [(b, b ^ 1) for b in range(lax.axis_size("blk"))])


def up(x):
    return lax.ppermute(x, "blk", z_shift(lax.axis_size("blk"), 1))


def down(x):
    return lax.ppermute(x, "blk", z_shift(lax.axis_size("blk"), -1))


def owner_at(offset, flip):
    half = lax.axis_size("blk") // 2
    me = lax.axis_index("blk")
    return (me // 2 + offset + half) % half * 2 + (me % 2 + flip) % 2


def owner_table():
    return jnp.stack([owner_at(*o) for stage in STAGES for o in stage]).astype(jnp.int32)


def gather_run(x, run):
    rows = x.shape[0]
    bases = [sum(len(s) for s in STAGES[:i]) for i in range(len(STAGES))]
    other, ahead, back = y_swap(x), up(x), down(x)
    shards = {(0, 0): (x, 0), (0, 1): (other, 0), (-1, 0): (ahead, 0), (1, 0): (back, 0)}
    ahead2, back2 = up(other), down(other)
    result = run(None, STAGES[0], bases[0], shards)
    ahead2, back2, result = lax.optimization_barrier((ahead2, back2, result))
    shards[-1, 1], shards[1, 1] = (ahead2, 0), (back2, 0)
    ahead, back = jnp.concatenate([ahead, ahead2]), jnp.concatenate([back, back2])
    for step in (2, 3):
        ahead, back = up(ahead), down(back)
        if step == 3:
            result = run(result, STAGES[1], bases[1], shards)
            ahead, back, result = lax.optimization_barrier((ahead, back, result))
        for flip in (0, 1):
            shards[-step, flip] = (ahead, flip * rows)
            shards[step, flip] = (back, flip * rows)
    shards[4, 0], shards[4, 1] = (up(ahead[:rows]), 0), (down(back[rows:]), 0)
    for stage, base in zip(STAGES[2:], bases[2:]):
        result = run(result, stage, base, shards)
    return result


def stage_pieces(shards, stage, rows):
    arrays, moves = [], []
    for k, owner in enumerate(stage):
        array, source = shards[owner]
        at = [i for i, a in enumerate(arrays) if a is array]
        if not at:
            at = [len(arrays)]
            arrays.append(array)
        moves.append((at[0], source, k * rows, rows))
    return arrays, moves


def start_moves(moves, pieces, slab, sems):
    copies = [
        pltpu.make_async_copy(
            pieces[a].at[pl.ds(source, count)], slab.at[pl.ds(target, count)], sems.at[i]
        )
        for i, (a, source, target, count) in enumerate(moves)
    ]
    for copy in copies:
        copy.start()
    return copies


def product_kernel(moves, arrays, base, owned, columns, *refs):
    owners, order, cols, weights, values = refs[:5]
    pieces = refs[5 : 5 + arrays]
    out, slab, blocks, results, slab_sems, block_sems, out_sems = refs[-7:]
    arrive = start_moves(moves, pieces, slab, slab_sems)
    which, loads = [], []
    for k in range(blocks.shape[0]):
        at = order[owners[base + k // owned] * owned + k % owned]
        which.append(at)
        loads.append(pltpu.make_async_copy(values.at[at], blocks.at[k], block_sems.at[k]))
        loads[-1].start()
    for copy in arrive:
        copy.wait()
    stores = []
    for low in range(0, len(which), owned):
        group = range(low, low + owned)
        for k in group:
            loads[k].wait()
        for k in group:
            place = k // owned * columns + lax.rem(cols[which[k]], columns)
            product = jnp.dot(blocks[k], slab[place], preferred_element_type=jnp.float32)
            results[k] = product * weights[which[k]]
        for k in group:
            stores.append(pltpu.make_async_copy(results.at[k], out.at[which[k]], out_sems.at[k]))
            stores[-1].start()
    for copy in stores:
        copy.wait()


def products(values, order, cols, weights, shard, columns):
    blocks, side = values.shape[:2]
    owned = blocks // lax.axis_size("blk")
    owners = owner_table()

    def run(result, stage, base, shards):
        arrays, moves = stage_pieces(shards, stage, columns)
        width, count = arrays[0].shape[2], len(stage) * owned
        smem, hbm = pl.BlockSpec(memory_space=pltpu.SMEM), pl.BlockSpec(memory_space=pl.ANY)
        operands = [owners, order, cols, weights, values, *arrays]
        aliases = {}
        if result is not None:
            aliases = {len(operands): 0}
            operands.append(result)
        return pl.pallas_call(
            functools.partial(product_kernel, moves, len(arrays), base, owned, columns),
            out_shape=jax.ShapeDtypeStruct((blocks, side, width), jnp.float32),
            in_specs=[smem] * 4 + [hbm] * (len(operands) - 4),
            out_specs=hbm,
            scratch_shapes=[
                pltpu.VMEM((len(stage) * columns, side, width), arrays[0].dtype),
                pltpu.VMEM((count, side, side), values.dtype),
                pltpu.VMEM((count, side, width), jnp.float32),
                pltpu.SemaphoreType.DMA((len(moves),)),
                pltpu.SemaphoreType.DMA((count,)),
                pltpu.SemaphoreType.DMA((count,)),
            ],
            input_output_aliases=aliases,
            compiler_params=pltpu.CompilerParams(vmem_limit_bytes=VMEM),
            cost_estimate=cost(count << 20),
        )(*operands)

    return gather_run(shard, run)


def combine_kernel(quads, modes, place, products_ref, *refs):
    out_ref = refs[-1]
    for g in range(quads):
        at = place[1] + g
        blocks = [products_ref[0, at * QUAD + i] for i in range(QUAD)]
        for ref, mode in zip(refs, modes):
            if mode == "whole" or mode == "same" or mode == ("first", "last")[g]:
                index = {"whole": at, "same": g}.get(mode, 0)
                scales = quad_scales(ref, index)
                for i in range(QUAD):
                    blocks[i] += quad_code(ref, index, i) * scales[i : i + 1]
        put_quad(out_ref, g, blocks)


def combine(products_, chunk, first, quads, *terms):
    tall, width = QUAD * products_.shape[2] + META, products_.shape[3]
    place = jnp.stack([jnp.asarray(chunk, jnp.int32), jnp.asarray(first, jnp.int32)])
    arrays = [array for array, _ in terms]
    return pl.pallas_call(
        functools.partial(combine_kernel, quads, [mode for _, mode in terms]),
        out_shape=jax.ShapeDtypeStruct((quads, tall, width), jnp.int16),
        grid_spec=pltpu.PrefetchScalarGridSpec(
            num_scalar_prefetch=1,
            grid=(1,),
            in_specs=[pl.BlockSpec((1,) + products_.shape[1:], lambda s, p: (p[0], 0, 0, 0))]
            + [pl.BlockSpec(a.shape, lambda s, p: (0, 0, 0)) for a in arrays],
            out_specs=pl.BlockSpec((quads, tall, width), lambda s, p: (0, 0, 0)),
        ),
        compiler_params=pltpu.CompilerParams(vmem_limit_bytes=VMEM),
        cost_estimate=cost(8 << 20),
    )(place, products_, *arrays)


def row_sums(product):
    half = lax.axis_size("blk") // 2
    me = lax.axis_index("blk")
    z, y = me // 2, me % 2
    product = product.reshape((half, product.shape[0] // half) + product.shape[1:])

    def chunk(offset):
        return (z + offset + half) % half

    a = up(combine(product, chunk(4), 0, 1))
    b = down(combine(product, chunk(4), 1, 1))
    a = up(combine(product, chunk(3), 0, 2, (a, "first")))
    b = down(combine(product, chunk(-3), 0, 2, (b, "last")))
    for step in (2, 1):
        a = up(combine(product, chunk(step), 0, 2, (a, "whole")))
        b = down(combine(product, chunk(-step), 0, 2, (b, "whole")))
    other = y_swap(combine(product, z, 1 - y, 1, (a, "whole"), (b, "whole")))
    return combine(product, z, y, 1, (a, "whole"), (b, "whole"), (other, "same"))


def contrib_kernel(moves, arrays, base, owned, columns, *refs):
    owners, rank, cols, weights, values = refs[:5]
    pieces = refs[5 : 5 + arrays]
    out, slab, blocks, results, slab_sems, block_sems, out_sems = refs[-7:]
    arrive = start_moves(moves, pieces, slab, slab_sems)
    firsts, loads = [], []
    for k in range(blocks.shape[0] // owned):
        firsts.append(owners[base + k] * owned)
        loads.append(
            pltpu.make_async_copy(
                values.at[pl.ds(firsts[k], owned)],
                blocks.at[pl.ds(k * owned, owned)],
                block_sems.at[k],
            )
        )
        loads[-1].start()
    for copy in arrive:
        copy.wait()
    stores = []
    for k, first in enumerate(firsts):
        loads[k].wait()
        found = []
        scales = quad_scales(slab, k)
        for i in range(owned):
            code = quad_code(slab, k, i)
            high = code.astype(jnp.bfloat16)
            low = (code - high.astype(jnp.float32)).astype(jnp.bfloat16)
            both = jnp.concatenate([high, low], axis=1)
            product = lax.dot_general(
                blocks[k * owned + i],
                both,
                (((0,), (0,)), ((), ())),
                preferred_element_type=jnp.float32,
            )
            width = high.shape[1]
            weight = scales[i : i + 1] * weights[first + i]
            found.append((product[:, :width] + product[:, width:]) * weight)
        extras = [lax.rem(cols[first + i], columns) for i in range(owned)]
        put_coded(results, k * owned, found, extras)
        for i in range(owned):
            slot = k * owned + i
            stores.append(
                pltpu.make_async_copy(
                    results.at[slot], out.at[rank[first + i]], out_sems.at[slot]
                )
            )
            stores[-1].start()
    for copy in stores:
        copy.wait()


def contribs(values, rank, cols, weights, shard, columns):
    blocks, side = values.shape[:2]
    owned = blocks // lax.axis_size("blk")
    owners = owner_table()

    def run(result, stage, base, shards):
        arrays, moves = stage_pieces(shards, stage, 1)
        quad, width = arrays[0].shape[1:]
        tall = side + META
        count = len(stage) * owned
        smem, hbm = pl.BlockSpec(memory_space=pltpu.SMEM), pl.BlockSpec(memory_space=pl.ANY)
        operands = [owners, rank, cols, weights, values, *arrays]
        aliases = {}
        if result is not None:
            aliases = {len(operands): 0}
            operands.append(result)
        return pl.pallas_call(
            functools.partial(contrib_kernel, moves, len(arrays), base, owned, columns),
            out_shape=jax.ShapeDtypeStruct((blocks, tall, width), jnp.int16),
            in_specs=[smem] * 4 + [hbm] * (len(operands) - 4),
            out_specs=hbm,
            scratch_shapes=[
                pltpu.VMEM((len(stage), quad, width), jnp.int16),
                pltpu.VMEM((count, side, side), values.dtype),
                pltpu.VMEM((count, tall, width), jnp.int16),
                pltpu.SemaphoreType.DMA((len(moves),)),
                pltpu.SemaphoreType.DMA((len(stage),)),
                pltpu.SemaphoreType.DMA((count,)),
            ],
            input_output_aliases=aliases,
            compiler_params=pltpu.CompilerParams(vmem_limit_bytes=VMEM),
            cost_estimate=cost(count << 20),
        )(*operands)

    return gather_run(shard, run)


def three_parts(x):
    high = x.astype(jnp.bfloat16)
    rest = x - high.astype(jnp.float32)
    middle = rest.astype(jnp.bfloat16)
    return high, middle, (rest - middle.astype(jnp.float32)).astype(jnp.bfloat16)


def dot_down(a, b):
    return lax.dot_general(a, b, (((0,), (0,)), ((), ())), preferred_element_type=jnp.float32)


def column_kernel(slots, in_ref, out_ref, gram_ref):
    step = pl.program_id(0)
    count = in_ref.shape[0]

    @pl.when(step == 0)
    def _():
        out_ref[...] = jnp.zeros_like(out_ref)

    for i in range(count):
        slot = slots[step * count + i]
        out_ref[slot] += decoded(in_ref, i)

    @pl.when(step == pl.num_programs(0) - 1)
    def _():
        width = gram_ref.shape[0]
        main = jnp.zeros((2 * width, 2 * width), jnp.float32)
        rest = jnp.zeros((width, width), jnp.float32)
        for c in range(out_ref.shape[0]):
            high, middle, low = three_parts(out_ref[c])
            pair = jnp.concatenate([high, middle], axis=1)
            main += dot_down(pair, pair)
            rest += dot_down(high, low)
        rest += main[:width, width:]
        gram_ref[...] = main[:width, :width] + (rest + rest.T + main[width:, width:])


def column_sums(parts, slots, columns):
    blocks, tall, width = parts.shape
    batch = 16
    return pl.pallas_call(
        column_kernel,
        out_shape=(
            jax.ShapeDtypeStruct((columns, tall - META, width), jnp.float32),
            jax.ShapeDtypeStruct((width, width), jnp.float32),
        ),
        grid_spec=pltpu.PrefetchScalarGridSpec(
            num_scalar_prefetch=1,
            grid=(blocks // batch,),
            in_specs=[pl.BlockSpec((batch, tall, width), lambda s, *_: (s, 0, 0))],
            out_specs=(
                pl.BlockSpec((columns, tall - META, width), lambda s, *_: (0, 0, 0)),
                pl.BlockSpec((width, width), lambda s, *_: (0, 0)),
            ),
        ),
        compiler_params=pltpu.CompilerParams(vmem_limit_bytes=VMEM),
    )(slots, parts)


def gram_total(gram):
    size = gram.shape[0]
    parts = lax.axis_size("row")
    some = lax.all_to_all(gram, "row", 0, 0, tiled=True)
    some = jnp.sum(some.reshape(parts, size // parts, size), axis=0)
    count = lax.axis_size("blk")
    some = jnp.broadcast_to(some[None], (count,) + some.shape)
    some = jnp.sum(lax.all_to_all(some, "blk", 0, 0, tiled=True), axis=0)
    some = jnp.broadcast_to(some[None], (parts,) + some.shape)
    return lax.all_to_all(some, "row", 0, 0, tiled=True).reshape(size, size)


PANEL = 32
GROUP = 4


def inverse_root(x):
    y = lax.rsqrt(x)
    return y * (1.5 - 0.5 * x * y * y)


def eliminate(panel, other, first, down):
    size = panel.shape[1]
    for q in range(0, PANEL, GROUP):
        j = first + q
        columns = [jnp.broadcast_to(panel[:, j + b : j + b + 1], panel.shape) for b in range(GROUP)]
        rows = [panel[q + a : q + a + 1] for a in range(GROUP)]
        others = [other[q + a : q + a + 1] for a in range(GROUP)]
        lower, inverse = {}, []
        for b in range(GROUP):
            for c in range(b, GROUP):
                entry = columns[c][q + b : q + b + 1]
                for k in range(b):
                    entry = entry - lower[b, k] * lower[c, k]
                if c == b:
                    inverse.append(inverse_root(entry))
                else:
                    lower[c, b] = entry * inverse[b]
        for b in range(GROUP):
            for k in range(b):
                rows[b] = rows[b] - lower[b, k] * rows[k]
                others[b] = others[b] - lower[b, k] * others[k]
                columns[b] = columns[b] - lower[b, k] * columns[k]
            rows[b] = rows[b] * inverse[b]
            others[b] = others[b] * inverse[b]
            columns[b] = columns[b] * inverse[b]
        if q + GROUP < PANEL:
            below = down >= q + GROUP
            change = sum(c * r for c, r in zip(columns, rows))
            panel = jnp.where(below, panel - change, panel)
            change = sum(c * r for c, r in zip(columns, others))
            other = jnp.where(below, other - change, other)
        for b in range(GROUP):
            panel = jnp.where(down == q + b, rows[b], panel)
            other = jnp.where(down == q + b, others[b], other)
    across = lax.broadcasted_iota(jnp.int32, (PANEL, size), 1)
    return jnp.where(across >= down + first, panel, 0.0), other


def factor_kernel(gram_ref, sums_ref, basis_ref, upper_ref, g_ref, m_ref):
    size = gram_ref.shape[0]
    down = lax.broadcasted_iota(jnp.int32, (PANEL, size), 0)
    g_ref[...] = gram_ref[...] * (1.0 / (NCB * BS))
    m_ref[...] = (
        lax.broadcasted_iota(jnp.int32, (size, size), 0)
        == lax.broadcasted_iota(jnp.int32, (size, size), 1)
    ).astype(jnp.float32)
    for first in range(0, size, PANEL):
        here, after = pl.ds(first, PANEL), pl.ds(first + PANEL, size - first - PANEL)
        panel, other = eliminate(g_ref[here, :], m_ref[here, :], first, down)
        upper_ref[here, :] = panel
        m_ref[here, :] = other
        if first + PANEL < size:
            high, middle, low = three_parts(panel)
            left = jnp.concatenate([high, middle, high, middle, high, low], axis=0)
            high, middle, low = three_parts(jnp.concatenate([panel, other], axis=1))
            right = jnp.concatenate([high, high, middle, middle, low, high], axis=0)
            update = dot_down(left, right)[first + PANEL :]
            g_ref[after, :] -= update[:, :size]
            m_ref[after, :] -= update[:, size:]
    high, middle, low = three_parts(m_ref[...].T)
    main = jnp.concatenate([jnp.concatenate([high, middle], axis=1)] * 2, axis=0)
    rest = jnp.concatenate([low, high], axis=0)
    for c in range(sums_ref.shape[0]):
        high, middle, low = three_parts(sums_ref[c])
        first = jnp.dot(
            jnp.concatenate([high, middle], axis=1), main, preferred_element_type=jnp.float32
        )
        second = jnp.dot(
            jnp.concatenate([high, low], axis=1), rest, preferred_element_type=jnp.float32
        )
        basis_ref[c] = first[:, :size] + (first[:, size:] + second)


def factor(gram, sums):
    return pl.pallas_call(
        factor_kernel,
        out_shape=(
            jax.ShapeDtypeStruct(sums.shape, jnp.float32),
            jax.ShapeDtypeStruct(gram.shape, jnp.float32),
        ),
        in_specs=[pl.BlockSpec(memory_space=pltpu.VMEM)] * 2,
        out_specs=(pl.BlockSpec(memory_space=pltpu.VMEM),) * 2,
        scratch_shapes=[pltpu.VMEM(gram.shape, jnp.float32)] * 2,
        compiler_params=pltpu.CompilerParams(vmem_limit_bytes=VMEM),
    )(gram, sums)


def local(values, scales, pattern, omega):
    blocks = pattern.size
    columns, side, width = omega.shape
    parts = lax.axis_size("blk")
    values = values.reshape(blocks, side, side)
    cols = pattern.reshape(-1) - lax.axis_index("row") * columns * parts
    weights = scales.astype(jnp.float32).reshape(-1)
    count = lax.iota(jnp.int32, blocks)
    key = cols * blocks + count
    rank = jnp.sum((key[None, :] < key[:, None]).astype(jnp.int32), axis=1)
    order = jnp.sum(jnp.where(rank[None, :] == count[:, None], count[None, :], 0), axis=1)

    product = products(values, order, cols, weights, omega, columns)
    rowvec = row_sums(product)
    coded = contribs(values, rank, cols, weights, rowvec, columns)
    coded = lax.all_to_all(coded, "blk", 0, 0, tiled=True)
    sums, gram = column_sums(coded, coded[:, side + 2, 0].astype(jnp.int32), columns)
    return factor(gram_total(gram), sums)


def solution(mesh):
    return jax.shard_map(
        local,
        mesh=mesh,
        in_specs=(
            P("row", "blk", None, None),
            P("row", "blk"),
            P("row", "blk"),
            P(("row", "blk"), None, None),
        ),
        out_specs=(P(("row", "blk"), None, None), P()),
        check_vma=False,
    )
```

```python
import functools

import jax
import jax.numpy as jnp
from jax import lax
from jax.experimental import pallas as pl
from jax.experimental.pallas import tpu as pltpu
from jax.sharding import PartitionSpec as P

BS = 256
NCB = 2048
META = 16
TOP = 32700.0
QUAD = 4
VMEM = 16 * 1024 * 1024


def codes_of(blocks):
    tops = [jnp.max(jnp.abs(x), axis=0, keepdims=True) for x in blocks]
    top = jnp.concatenate(tops, axis=0)
    expo = jnp.clip(jnp.ceil(jnp.log2(jnp.maximum(top, 1e-30))), -90.0, 120.0)
    small = jnp.exp2(-expo)
    frac = jnp.minimum(jnp.ceil(top * small * 256.0 + 0.5), 300.0)
    inverse = TOP * 256.0 * small / frac
    codes = [
        jnp.round(x * inverse[i : i + 1]).astype(jnp.int32).astype(jnp.int16)
        for i, x in enumerate(blocks)
    ]
    return codes, expo.astype(jnp.int32), frac.astype(jnp.int32)


def put_coded(ref, base, blocks, extras):
    rows, width = blocks[0].shape
    codes, expo, frac = codes_of(blocks)
    place = lax.broadcasted_iota(jnp.int32, (META, width), 0)
    for i, code in enumerate(codes):
        ref[base + i, pl.ds(0, rows)] = code
        meta = jnp.where(place == 0, expo[i : i + 1], frac[i : i + 1])
        meta = jnp.where(place == 2, extras[i], meta)
        ref[base + i, pl.ds(rows, META)] = meta.astype(jnp.int16)


def put_quad(ref, index, blocks):
    rows, width = blocks[0].shape
    codes, expo, frac = codes_of(blocks)
    for i, code in enumerate(codes):
        ref[index, pl.ds(i * rows, rows)] = code
    spare = jnp.zeros((META - 2 * QUAD, width), jnp.int32)
    meta = jnp.concatenate([expo, frac, spare], axis=0)
    ref[index, pl.ds(QUAD * rows, META)] = meta.astype(jnp.int16)


def quad_scales(ref, index):
    meta = ref[index, pl.ds(ref.shape[1] - META, META)].astype(jnp.int32).astype(jnp.float32)
    return jnp.exp2(meta[:QUAD]) * meta[QUAD : 2 * QUAD] * (1.0 / (256.0 * TOP))


def quad_code(ref, index, i):
    rows = (ref.shape[1] - META) // QUAD
    return ref[index, pl.ds(i * rows, rows)].astype(jnp.int32).astype(jnp.float32)


def scale_of(meta):
    meta = meta.astype(jnp.int32).astype(jnp.float32)
    return jnp.exp2(meta[0:1]) * meta[1:2] * (1.0 / (256.0 * TOP))


def decoded(ref, index):
    rows = ref.shape[1] - META
    code = ref[index, pl.ds(0, rows)].astype(jnp.int32).astype(jnp.float32)
    return code * scale_of(ref[index, pl.ds(rows, META)])


def cost(size):
    return pl.CostEstimate(flops=0, bytes_accessed=size, transcendentals=0)


STAGES = (
    ((0, 0), (-1, 0), (1, 0)),
    ((0, 1), (-1, 1), (1, 1), (-2, 0), (2, 0)),
    ((-3, 0), (3, 0)),
    ((-2, 1), (2, 1), (-3, 1), (3, 1), (4, 0)),
    ((4, 1),),
)


def z_shift(size, step):
    half = size // 2
    return [(z * 2 + y, (z + step) % half * 2 + y) for z in range(half) for y in range(2)]


def y_swap(x):
    return lax.ppermute(x, "blk", [(b, b ^ 1) for b in range(lax.axis_size("blk"))])


def up(x):
    return lax.ppermute(x, "blk", z_shift(lax.axis_size("blk"), 1))


def down(x):
    return lax.ppermute(x, "blk", z_shift(lax.axis_size("blk"), -1))


def owner_at(offset, flip):
    half = lax.axis_size("blk") // 2
    me = lax.axis_index("blk")
    return (me // 2 + offset + half) % half * 2 + (me % 2 + flip) % 2


def owner_table():
    return jnp.stack([owner_at(*o) for stage in STAGES for o in stage]).astype(jnp.int32)


def gather_run(x, early, run):
    rows = x.shape[0]
    late = rows - early
    shards = {}

    def put(offset, flip, array):
        shards.setdefault((offset, flip), []).append((array, 0, 0, array.shape[0]))

    def swap_tails(*offsets):
        if late:
            tails = [shards[o, 0][0][0][-late:] for o in offsets]
            swapped = y_swap(jnp.concatenate(tails) if len(tails) > 1 else tails[0])
            for i, o in enumerate(offsets):
                shards.setdefault((o, 1), []).append((swapped, i * late, early, late))

    put(0, 0, x)
    other = y_swap(x[:early] if late else x)
    put(0, 1, other)
    ahead, back = up(x), down(x)
    put(-1, 0, ahead)
    put(1, 0, back)
    swap_tails(0, -1, 1)
    ahead2, back2 = other, other
    result, base = None, 0
    for step in (1, 2, 3):
        if step < 3:
            ahead, back = up(ahead), down(back)
            put(-1 - step, 0, ahead)
            put(1 + step, 0, back)
        else:
            put(4, 0, up(ahead))
        ahead2, back2 = up(ahead2), down(back2)
        result = run(result, STAGES[step - 1], base, shards)
        base += len(STAGES[step - 1])
        ahead2, back2, result = lax.optimization_barrier((ahead2, back2, result))
        put(-step, 1, ahead2)
        put(step, 1, back2)
        if step > 1:
            swap_tails(*((-2, 2, -3, 3) if step == 2 else (4,)))
    put(4, 1, down(back2))
    for stage in STAGES[3:]:
        result = run(result, stage, base, shards)
        base += len(stage)
    return result


def stage_pieces(shards, stage, rows):
    arrays, moves = [], []
    for k, owner in enumerate(stage):
        for array, source, first, count in shards[owner]:
            at = [i for i, a in enumerate(arrays) if a is array]
            if not at:
                at = [len(arrays)]
                arrays.append(array)
            moves.append((at[0], source, k * rows + first, count))
    return arrays, moves


def start_moves(moves, pieces, slab, sems):
    copies = [
        pltpu.make_async_copy(
            pieces[a].at[pl.ds(source, count)], slab.at[pl.ds(target, count)], sems.at[i]
        )
        for i, (a, source, target, count) in enumerate(moves)
    ]
    for copy in copies:
        copy.start()
    return copies


def product_kernel(moves, arrays, base, owned, columns, *refs):
    owners, order, cols, weights, values = refs[:5]
    pieces = refs[5 : 5 + arrays]
    out, slab, blocks, results, slab_sems, block_sems, out_sems = refs[-7:]
    arrive = start_moves(moves, pieces, slab, slab_sems)
    which, loads = [], []
    for k in range(blocks.shape[0]):
        at = order[owners[base + k // owned] * owned + k % owned]
        which.append(at)
        loads.append(pltpu.make_async_copy(values.at[at], blocks.at[k], block_sems.at[k]))
        loads[-1].start()
    for copy in arrive:
        copy.wait()
    stores = []
    for low in range(0, len(which), owned):
        group = range(low, low + owned)
        for k in group:
            loads[k].wait()
        for k in group:
            place = k // owned * columns + lax.rem(cols[which[k]], columns)
            product = jnp.dot(blocks[k], slab[place], preferred_element_type=jnp.float32)
            results[k] = product * weights[which[k]]
        for k in group:
            stores.append(pltpu.make_async_copy(results.at[k], out.at[which[k]], out_sems.at[k]))
            stores[-1].start()
    for copy in stores:
        copy.wait()


def products(values, order, cols, weights, shard, early, columns):
    blocks, side = values.shape[:2]
    owned = blocks // lax.axis_size("blk")
    owners = owner_table()

    def run(result, stage, base, shards):
        arrays, moves = stage_pieces(shards, stage, columns)
        width, count = arrays[0].shape[2], len(stage) * owned
        smem, hbm = pl.BlockSpec(memory_space=pltpu.SMEM), pl.BlockSpec(memory_space=pl.ANY)
        operands = [owners, order, cols, weights, values, *arrays]
        aliases = {}
        if result is not None:
            aliases = {len(operands): 0}
            operands.append(result)
        return pl.pallas_call(
            functools.partial(product_kernel, moves, len(arrays), base, owned, columns),
            out_shape=jax.ShapeDtypeStruct((blocks, side, width), jnp.float32),
            in_specs=[smem] * 4 + [hbm] * (len(operands) - 4),
            out_specs=hbm,
            scratch_shapes=[
                pltpu.VMEM((len(stage) * columns, side, width), arrays[0].dtype),
                pltpu.VMEM((count, side, side), values.dtype),
                pltpu.VMEM((count, side, width), jnp.float32),
                pltpu.SemaphoreType.DMA((len(moves),)),
                pltpu.SemaphoreType.DMA((count,)),
                pltpu.SemaphoreType.DMA((count,)),
            ],
            input_output_aliases=aliases,
            compiler_params=pltpu.CompilerParams(vmem_limit_bytes=VMEM),
            cost_estimate=cost(count << 20),
        )(*operands)

    return gather_run(shard, early, run)


def combine_kernel(offset, firsts, modes, place, products_ref, *refs):
    terms, out = refs[: len(modes)], refs[len(modes)]
    blocks, coded, results, block_sems, coded_sems, out_sems = refs[len(modes) + 1 :]
    half = products_ref.shape[0]
    chunk = lax.rem(place[0] + offset + half, half)
    loads = []
    for g, first in enumerate(firsts):
        at = {"mine": place[1], "other": 1 - place[1]}.get(first, first)
        copies = [
            pltpu.make_async_copy(
                products_ref.at[chunk, pl.ds(at * QUAD, QUAD)], blocks.at[g], block_sems.at[g]
            )
        ]
        slots = []
        for t, mode in enumerate(modes):
            if mode == "whole" or mode == "single" or mode == g:
                slots.append(t * len(firsts) + g)
                source = terms[t].at[at if mode == "whole" else 0]
                copies.append(
                    pltpu.make_async_copy(source, coded.at[slots[-1]], coded_sems.at[slots[-1]])
                )
        for copy in copies:
            copy.start()
        loads.append((copies, slots))
    stores = []
    for g, (copies, slots) in enumerate(loads):
        for copy in copies:
            copy.wait()
        found = [blocks[g, i] for i in range(QUAD)]
        for slot in slots:
            scales = quad_scales(coded, slot)
            for i in range(QUAD):
                found[i] += quad_code(coded, slot, i) * scales[i : i + 1]
        put_quad(results, g, found)
        stores.append(pltpu.make_async_copy(results.at[g], out.at[g], out_sems.at[g]))
        stores[-1].start()
    for copy in stores:
        copy.wait()


def combine(product, place, offset, firsts, *terms):
    side, width = product.shape[2:]
    tall, quads = QUAD * side + META, len(firsts)
    room = max(1, len(terms) * quads)
    hbm = pl.BlockSpec(memory_space=pl.ANY)
    return pl.pallas_call(
        functools.partial(combine_kernel, offset, firsts, [mode for _, mode in terms]),
        out_shape=jax.ShapeDtypeStruct((quads, tall, width), jnp.int16),
        in_specs=[pl.BlockSpec(memory_space=pltpu.SMEM)] + [hbm] * (1 + len(terms)),
        out_specs=hbm,
        scratch_shapes=[
            pltpu.VMEM((quads, QUAD, side, width), jnp.float32),
            pltpu.VMEM((room, tall, width), jnp.int16),
            pltpu.VMEM((quads, tall, width), jnp.int16),
            pltpu.SemaphoreType.DMA((quads,)),
            pltpu.SemaphoreType.DMA((room,)),
            pltpu.SemaphoreType.DMA((quads,)),
        ],
        compiler_params=pltpu.CompilerParams(vmem_limit_bytes=VMEM),
        cost_estimate=cost(8 << 20),
    )(place, product, *[array for array, _ in terms])


def row_sums(product):
    half = lax.axis_size("blk") // 2
    me = lax.axis_index("blk")
    place = jnp.stack([me // 2, me % 2]).astype(jnp.int32)
    product = product.reshape((half, product.shape[0] // half) + product.shape[1:])
    a = up(combine(product, place, 4, (0,)))
    b = down(combine(product, place, -4, (1,)))
    a = up(combine(product, place, 3, (0, 1), (a, 0)))
    b = down(combine(product, place, -3, (0, 1), (b, 1)))
    for step in (2, 1):
        a = up(combine(product, place, step, (0, 1), (a, "whole")))
        b = down(combine(product, place, -step, (0, 1), (b, "whole")))
    terms = ((a, "whole"), (b, "whole"))
    other = y_swap(combine(product, place, 0, ("other",), *terms))
    return combine(product, place, 0, ("mine",), *terms, (other, "single"))


def contrib_kernel(moves, arrays, base, owned, columns, *refs):
    owners, rank, cols, weights, values = refs[:5]
    pieces = refs[5 : 5 + arrays]
    out, slab, blocks, results, slab_sems, block_sems, out_sems = refs[-7:]
    arrive = start_moves(moves, pieces, slab, slab_sems)
    firsts, loads = [], []
    for k in range(blocks.shape[0] // owned):
        firsts.append(owners[base + k] * owned)
        loads.append(
            pltpu.make_async_copy(
                values.at[pl.ds(firsts[k], owned)],
                blocks.at[pl.ds(k * owned, owned)],
                block_sems.at[k],
            )
        )
        loads[-1].start()
    for copy in arrive:
        copy.wait()
    stores = []
    for k, first in enumerate(firsts):
        loads[k].wait()
        found = []
        scales = quad_scales(slab, k)
        for i in range(owned):
            code = quad_code(slab, k, i)
            high = code.astype(jnp.bfloat16)
            low = (code - high.astype(jnp.float32)).astype(jnp.bfloat16)
            both = jnp.concatenate([high, low], axis=1)
            product = lax.dot_general(
                blocks[k * owned + i],
                both,
                (((0,), (0,)), ((), ())),
                preferred_element_type=jnp.float32,
            )
            width = high.shape[1]
            weight = scales[i : i + 1] * weights[first + i]
            found.append((product[:, :width] + product[:, width:]) * weight)
        extras = [lax.rem(cols[first + i], columns) for i in range(owned)]
        put_coded(results, k * owned, found, extras)
        for i in range(owned):
            slot = k * owned + i
            stores.append(
                pltpu.make_async_copy(
                    results.at[slot], out.at[rank[first + i]], out_sems.at[slot]
                )
            )
            stores[-1].start()
    for copy in stores:
        copy.wait()


def contribs(values, rank, cols, weights, shard, early, columns):
    blocks, side = values.shape[:2]
    owned = blocks // lax.axis_size("blk")
    owners = owner_table()

    def run(result, stage, base, shards):
        arrays, moves = stage_pieces(shards, stage, 1)
        quad, width = arrays[0].shape[1:]
        tall = side + META
        count = len(stage) * owned
        smem, hbm = pl.BlockSpec(memory_space=pltpu.SMEM), pl.BlockSpec(memory_space=pl.ANY)
        operands = [owners, rank, cols, weights, values, *arrays]
        aliases = {}
        if result is not None:
            aliases = {len(operands): 0}
            operands.append(result)
        return pl.pallas_call(
            functools.partial(contrib_kernel, moves, len(arrays), base, owned, columns),
            out_shape=jax.ShapeDtypeStruct((blocks, tall, width), jnp.int16),
            in_specs=[smem] * 4 + [hbm] * (len(operands) - 4),
            out_specs=hbm,
            scratch_shapes=[
                pltpu.VMEM((len(stage), quad, width), jnp.int16),
                pltpu.VMEM((count, side, side), values.dtype),
                pltpu.VMEM((count, tall, width), jnp.int16),
                pltpu.SemaphoreType.DMA((len(moves),)),
                pltpu.SemaphoreType.DMA((len(stage),)),
                pltpu.SemaphoreType.DMA((count,)),
            ],
            input_output_aliases=aliases,
            compiler_params=pltpu.CompilerParams(vmem_limit_bytes=VMEM),
            cost_estimate=cost(count << 20),
        )(*operands)

    return gather_run(shard, early, run)


def three_parts(x):
    high = x.astype(jnp.bfloat16)
    rest = x - high.astype(jnp.float32)
    middle = rest.astype(jnp.bfloat16)
    return high, middle, (rest - middle.astype(jnp.float32)).astype(jnp.bfloat16)


def dot_down(a, b):
    return lax.dot_general(a, b, (((0,), (0,)), ((), ())), preferred_element_type=jnp.float32)


def column_kernel(slots, in_ref, out_ref, gram_ref):
    step = pl.program_id(0)
    count = in_ref.shape[0]

    @pl.when(step == 0)
    def _():
        out_ref[...] = jnp.zeros_like(out_ref)

    for i in range(count):
        slot = slots[step * count + i]
        out_ref[slot] += decoded(in_ref, i)

    @pl.when(step == pl.num_programs(0) - 1)
    def _():
        width = gram_ref.shape[0]
        main = jnp.zeros((2 * width, 2 * width), jnp.float32)
        rest = jnp.zeros((width, width), jnp.float32)
        for c in range(out_ref.shape[0]):
            high, middle, low = three_parts(out_ref[c])
            pair = jnp.concatenate([high, middle], axis=1)
            main += dot_down(pair, pair)
            rest += dot_down(high, low)
        rest += main[:width, width:]
        gram_ref[...] = main[:width, :width] + (rest + rest.T + main[width:, width:])


def column_sums(parts, slots, columns):
    blocks, tall, width = parts.shape
    batch = 16
    return pl.pallas_call(
        column_kernel,
        out_shape=(
            jax.ShapeDtypeStruct((columns, tall - META, width), jnp.float32),
            jax.ShapeDtypeStruct((width, width), jnp.float32),
        ),
        grid_spec=pltpu.PrefetchScalarGridSpec(
            num_scalar_prefetch=1,
            grid=(blocks // batch,),
            in_specs=[pl.BlockSpec((batch, tall, width), lambda s, *_: (s, 0, 0))],
            out_specs=(
                pl.BlockSpec((columns, tall - META, width), lambda s, *_: (0, 0, 0)),
                pl.BlockSpec((width, width), lambda s, *_: (0, 0)),
            ),
        ),
        compiler_params=pltpu.CompilerParams(vmem_limit_bytes=VMEM),
    )(slots, parts)


def gram_total(gram):
    size = gram.shape[0]
    parts = lax.axis_size("row")
    some = lax.all_to_all(gram, "row", 0, 0, tiled=True)
    some = jnp.sum(some.reshape(parts, size // parts, size), axis=0)
    count = lax.axis_size("blk")
    some = jnp.broadcast_to(some[None], (count,) + some.shape)
    some = jnp.sum(lax.all_to_all(some, "blk", 0, 0, tiled=True), axis=0)
    some = jnp.broadcast_to(some[None], (parts,) + some.shape)
    return lax.all_to_all(some, "row", 0, 0, tiled=True).reshape(size, size)


PANEL = 32
GROUP = 4


def inverse_root(x):
    y = lax.rsqrt(x)
    return y * (1.5 - 0.5 * x * y * y)


def eliminate(panel, other, first, down):
    size = panel.shape[1]
    for q in range(0, PANEL, GROUP):
        j = first + q
        columns = [jnp.broadcast_to(panel[:, j + b : j + b + 1], panel.shape) for b in range(GROUP)]
        rows = [panel[q + a : q + a + 1] for a in range(GROUP)]
        others = [other[q + a : q + a + 1] for a in range(GROUP)]
        lower, inverse = {}, []
        for b in range(GROUP):
            for c in range(b, GROUP):
                entry = columns[c][q + b : q + b + 1]
                for k in range(b):
                    entry = entry - lower[b, k] * lower[c, k]
                if c == b:
                    inverse.append(inverse_root(entry))
                else:
                    lower[c, b] = entry * inverse[b]
        for b in range(GROUP):
            for k in range(b):
                rows[b] = rows[b] - lower[b, k] * rows[k]
                others[b] = others[b] - lower[b, k] * others[k]
                columns[b] = columns[b] - lower[b, k] * columns[k]
            rows[b] = rows[b] * inverse[b]
            others[b] = others[b] * inverse[b]
            columns[b] = columns[b] * inverse[b]
        if q + GROUP < PANEL:
            below = down >= q + GROUP
            change = sum(c * r for c, r in zip(columns, rows))
            panel = jnp.where(below, panel - change, panel)
            change = sum(c * r for c, r in zip(columns, others))
            other = jnp.where(below, other - change, other)
        for b in range(GROUP):
            panel = jnp.where(down == q + b, rows[b], panel)
            other = jnp.where(down == q + b, others[b], other)
    across = lax.broadcasted_iota(jnp.int32, (PANEL, size), 1)
    return jnp.where(across >= down + first, panel, 0.0), other


def factor_kernel(gram_ref, sums_ref, basis_ref, upper_ref, g_ref, m_ref):
    size = gram_ref.shape[0]
    down = lax.broadcasted_iota(jnp.int32, (PANEL, size), 0)
    g_ref[...] = gram_ref[...] * (1.0 / (NCB * BS))
    m_ref[...] = (
        lax.broadcasted_iota(jnp.int32, (size, size), 0)
        == lax.broadcasted_iota(jnp.int32, (size, size), 1)
    ).astype(jnp.float32)
    for first in range(0, size, PANEL):
        here, after = pl.ds(first, PANEL), pl.ds(first + PANEL, size - first - PANEL)
        panel, other = eliminate(g_ref[here, :], m_ref[here, :], first, down)
        upper_ref[here, :] = panel
        m_ref[here, :] = other
        if first + PANEL < size:
            high, middle, low = three_parts(panel)
            left = jnp.concatenate([high, middle, high, middle, high, low], axis=0)
            high, middle, low = three_parts(jnp.concatenate([panel, other], axis=1))
            right = jnp.concatenate([high, high, middle, middle, low, high], axis=0)
            update = dot_down(left, right)[first + PANEL :]
            g_ref[after, :] -= update[:, :size]
            m_ref[after, :] -= update[:, size:]
    high, middle, low = three_parts(m_ref[...].T)
    main = jnp.concatenate([jnp.concatenate([high, middle], axis=1)] * 2, axis=0)
    rest = jnp.concatenate([low, high], axis=0)
    for c in range(sums_ref.shape[0]):
        high, middle, low = three_parts(sums_ref[c])
        first = jnp.dot(
            jnp.concatenate([high, middle], axis=1), main, preferred_element_type=jnp.float32
        )
        second = jnp.dot(
            jnp.concatenate([high, low], axis=1), rest, preferred_element_type=jnp.float32
        )
        basis_ref[c] = first[:, :size] + (first[:, size:] + second)


def factor(gram, sums):
    return pl.pallas_call(
        factor_kernel,
        out_shape=(
            jax.ShapeDtypeStruct(sums.shape, jnp.float32),
            jax.ShapeDtypeStruct(gram.shape, jnp.float32),
        ),
        in_specs=[pl.BlockSpec(memory_space=pltpu.VMEM)] * 2,
        out_specs=(pl.BlockSpec(memory_space=pltpu.VMEM),) * 2,
        scratch_shapes=[pltpu.VMEM(gram.shape, jnp.float32)] * 2,
        compiler_params=pltpu.CompilerParams(vmem_limit_bytes=VMEM),
    )(gram, sums)


def local(values, scales, pattern, omega):
    blocks = pattern.size
    columns, side, width = omega.shape
    parts = lax.axis_size("blk")
    values = values.reshape(blocks, side, side)
    cols = pattern.reshape(-1) - lax.axis_index("row") * columns * parts
    weights = scales.astype(jnp.float32).reshape(-1)
    count = lax.iota(jnp.int32, blocks)
    key = cols * blocks + count
    rank = jnp.sum((key[None, :] < key[:, None]).astype(jnp.int32), axis=1)
    order = jnp.sum(jnp.where(rank[None, :] == count[:, None], count[None, :], 0), axis=1)

    product = products(values, order, cols, weights, omega, columns - columns // 4, columns)
    rowvec = row_sums(product)
    coded = contribs(values, rank, cols, weights, rowvec, rowvec.shape[0], columns)
    coded = lax.all_to_all(coded, "blk", 0, 0, tiled=True)
    sums, gram = column_sums(coded, coded[:, side + 2, 0].astype(jnp.int32), columns)
    return factor(gram_total(gram), sums)


def solution(mesh):
    return jax.shard_map(
        local,
        mesh=mesh,
        in_specs=(
            P("row", "blk", None, None),
            P("row", "blk"),
            P("row", "blk"),
            P(("row", "blk"), None, None),
        ),
        out_specs=(P(("row", "blk"), None, None), P()),
        check_vma=False,
    )
```

```python
import functools

import jax
import jax.numpy as jnp
from jax import lax
from jax.experimental import pallas as pl
from jax.experimental.pallas import tpu as pltpu
from jax.sharding import PartitionSpec as P

BS = 256
NCB = 2048
META = 16
TOP = 32700.0
QUAD = 4
VMEM = 24 * 1024 * 1024


def codes_of(blocks):
    tops = [jnp.max(jnp.abs(x), axis=0, keepdims=True) for x in blocks]
    top = jnp.concatenate(tops, axis=0)
    expo = jnp.clip(jnp.ceil(jnp.log2(jnp.maximum(top, 1e-30))), -90.0, 120.0)
    small = jnp.exp2(-expo)
    frac = jnp.minimum(jnp.ceil(top * small * 256.0 + 0.5), 300.0)
    inverse = TOP * 256.0 * small / frac
    codes = [
        jnp.round(x * inverse[i : i + 1]).astype(jnp.int32).astype(jnp.int16)
        for i, x in enumerate(blocks)
    ]
    return codes, expo.astype(jnp.int32), frac.astype(jnp.int32)


def put_coded(ref, base, blocks, extras):
    rows, width = blocks[0].shape
    codes, expo, frac = codes_of(blocks)
    place = lax.broadcasted_iota(jnp.int32, (META, width), 0)
    for i, code in enumerate(codes):
        ref[base + i, pl.ds(0, rows)] = code
        meta = jnp.where(place == 0, expo[i : i + 1], frac[i : i + 1])
        meta = jnp.where(place == 2, extras[i], meta)
        ref[base + i, pl.ds(rows, META)] = meta.astype(jnp.int16)


def put_quad(ref, index, blocks):
    rows, width = blocks[0].shape
    codes, expo, frac = codes_of(blocks)
    for i, code in enumerate(codes):
        ref[index, pl.ds(i * rows, rows)] = code
    spare = jnp.zeros((META - 2 * QUAD, width), jnp.int32)
    meta = jnp.concatenate([expo, frac, spare], axis=0)
    ref[index, pl.ds(QUAD * rows, META)] = meta.astype(jnp.int16)


def quad_scales(ref, index):
    meta = ref[index, pl.ds(ref.shape[1] - META, META)].astype(jnp.int32).astype(jnp.float32)
    return jnp.exp2(meta[:QUAD]) * meta[QUAD : 2 * QUAD] * (1.0 / (256.0 * TOP))


def quad_code(ref, index, i):
    rows = (ref.shape[1] - META) // QUAD
    return ref[index, pl.ds(i * rows, rows)].astype(jnp.int32).astype(jnp.float32)


def scale_of(meta):
    meta = meta.astype(jnp.int32).astype(jnp.float32)
    return jnp.exp2(meta[0:1]) * meta[1:2] * (1.0 / (256.0 * TOP))


def decoded(ref, index):
    rows = ref.shape[1] - META
    code = ref[index, pl.ds(0, rows)].astype(jnp.int32).astype(jnp.float32)
    return code * scale_of(ref[index, pl.ds(rows, META)])


def cost(size):
    return pl.CostEstimate(flops=0, bytes_accessed=size, transcendentals=0)


STAGES = (
    ((0, 0), (-1, 0), (1, 0)),
    ((0, 1), (-1, 1), (1, 1), (-2, 0), (2, 0)),
    ((-3, 0), (3, 0)),
    ((-2, 1), (2, 1), (-3, 1), (3, 1), (4, 0)),
    ((4, 1),),
)


def z_shift(size, step):
    half = size // 2
    return [(z * 2 + y, (z + step) % half * 2 + y) for z in range(half) for y in range(2)]


def y_swap(x):
    return lax.ppermute(x, "blk", [(b, b ^ 1) for b in range(lax.axis_size("blk"))])


def up(x):
    return lax.ppermute(x, "blk", z_shift(lax.axis_size("blk"), 1))


def down(x):
    return lax.ppermute(x, "blk", z_shift(lax.axis_size("blk"), -1))


def owner_at(offset, flip):
    half = lax.axis_size("blk") // 2
    me = lax.axis_index("blk")
    return (me // 2 + offset + half) % half * 2 + (me % 2 + flip) % 2


def owner_table():
    return jnp.stack([owner_at(*o) for stage in STAGES for o in stage]).astype(jnp.int32)


def gather_run(x, early, run):
    rows = x.shape[0]
    late = rows - early
    shards = {}

    def put(offset, flip, array):
        shards.setdefault((offset, flip), []).append((array, 0, 0, array.shape[0]))

    def swap_tails(*offsets):
        if late:
            tails = [shards[o, 0][0][0][-late:] for o in offsets]
            swapped = y_swap(jnp.concatenate(tails) if len(tails) > 1 else tails[0])
            for i, o in enumerate(offsets):
                shards.setdefault((o, 1), []).append((swapped, i * late, early, late))

    put(0, 0, x)
    other = y_swap(x[:early] if late else x)
    put(0, 1, other)
    ahead, back = up(x), down(x)
    put(-1, 0, ahead)
    put(1, 0, back)
    swap_tails(0, -1, 1)
    ahead2, back2 = other, other
    result, base = None, 0
    for step in (1, 2, 3):
        if step < 3:
            ahead, back = up(ahead), down(back)
            put(-1 - step, 0, ahead)
            put(1 + step, 0, back)
        else:
            put(4, 0, up(ahead))
        ahead2, back2 = up(ahead2), down(back2)
        result = run(result, STAGES[step - 1], base, shards)
        base += len(STAGES[step - 1])
        ahead2, back2, result = lax.optimization_barrier((ahead2, back2, result))
        put(-step, 1, ahead2)
        put(step, 1, back2)
        if step > 1:
            swap_tails(*((-2, 2, -3, 3) if step == 2 else (4,)))
    put(4, 1, down(back2))
    for stage in STAGES[3:]:
        result = run(result, stage, base, shards)
        base += len(stage)
    return result


def stage_pieces(shards, stage, rows):
    arrays, moves = [], []
    for k, owner in enumerate(stage):
        for array, source, first, count in shards[owner]:
            at = [i for i, a in enumerate(arrays) if a is array]
            if not at:
                at = [len(arrays)]
                arrays.append(array)
            moves.append((at[0], source, k * rows + first, count))
    return arrays, moves


def start_moves(moves, pieces, slab, sems):
    copies = [
        pltpu.make_async_copy(
            pieces[a].at[pl.ds(source, count)], slab.at[pl.ds(target, count)], sems.at[i]
        )
        for i, (a, source, target, count) in enumerate(moves)
    ]
    for copy in copies:
        copy.start()
    return copies


def product_kernel(moves, arrays, base, owned, columns, *refs):
    owners, order, cols, weights, values = refs[:5]
    pieces = refs[5 : 5 + arrays]
    out, picked, results, pick_sems, out_sems = refs[-5:]
    which = []
    for k in range(picked.shape[0]):
        at = order[owners[base + k // owned] * owned + k % owned]
        which.append(at)
    picks = []
    for k, at in enumerate(which):
        column = lax.rem(cols[at], columns)
        parts = [move for move in moves if move[2] // columns == k // owned]
        for a, source, target, count in parts:
            place = column - target % columns
            row = source + jnp.clip(place, 0, count - 1)
            copy = pltpu.make_async_copy(pieces[a].at[row], picked.at[k], pick_sems.at[k])
            if len(parts) == 1:
                copy.start()
            else:

                @pl.when((place >= 0) & (place < count))
                def _(copy=copy):
                    copy.start()

        picks.append(copy)
    stores = []
    for low in range(0, len(which), owned):
        group = range(low, low + owned)
        for k in group:
            picks[k].wait()
        for k in group:
            product = jnp.dot(values[which[k]], picked[k], preferred_element_type=jnp.float32)
            results[k] = product * weights[which[k]]
        for k in group:
            stores.append(pltpu.make_async_copy(results.at[k], out.at[which[k]], out_sems.at[k]))
            stores[-1].start()
    for copy in stores:
        copy.wait()


def products(values, order, cols, weights, shard, early, columns):
    blocks, side = values.shape[:2]
    owned = blocks // lax.axis_size("blk")
    owners = owner_table()

    def run(result, stage, base, shards):
        arrays, moves = stage_pieces(shards, stage, columns)
        width, count = arrays[0].shape[2], len(stage) * owned
        smem, hbm = pl.BlockSpec(memory_space=pltpu.SMEM), pl.BlockSpec(memory_space=pl.ANY)
        kept = pl.BlockSpec(memory_space=pltpu.VMEM)
        operands = [owners, order, cols, weights, values, *arrays]
        aliases = {}
        if result is not None:
            aliases = {len(operands): 0}
            operands.append(result)
        return pl.pallas_call(
            functools.partial(product_kernel, moves, len(arrays), base, owned, columns),
            out_shape=jax.ShapeDtypeStruct((blocks, side, width), jnp.float32),
            in_specs=[smem] * 4 + [kept] + [hbm] * (len(operands) - 5),
            out_specs=hbm,
            scratch_shapes=[
                pltpu.VMEM((count, side, width), arrays[0].dtype),
                pltpu.VMEM((count, side, width), jnp.float32),
                pltpu.SemaphoreType.DMA((count,)),
                pltpu.SemaphoreType.DMA((count,)),
            ],
            input_output_aliases=aliases,
            compiler_params=pltpu.CompilerParams(vmem_limit_bytes=VMEM),
            cost_estimate=cost(count << 20),
        )(*operands)

    return gather_run(shard, early, run)


def combine_kernel(offset, firsts, modes, place, products_ref, *refs):
    terms, out = refs[: len(modes)], refs[len(modes)]
    blocks, coded, results, block_sems, coded_sems, out_sems = refs[len(modes) + 1 :]
    half = products_ref.shape[0]
    chunk = lax.rem(place[0] + offset + half, half)
    loads = []
    for g, first in enumerate(firsts):
        at = {"mine": place[1], "other": 1 - place[1]}.get(first, first)
        copies = [
            pltpu.make_async_copy(
                products_ref.at[chunk, pl.ds(at * QUAD, QUAD)], blocks.at[g], block_sems.at[g]
            )
        ]
        slots = []
        for t, mode in enumerate(modes):
            if mode == "whole" or mode == "single" or mode == g:
                slots.append(t * len(firsts) + g)
                source = terms[t].at[at if mode == "whole" else 0]
                copies.append(
                    pltpu.make_async_copy(source, coded.at[slots[-1]], coded_sems.at[slots[-1]])
                )
        for copy in copies:
            copy.start()
        loads.append((copies, slots))
    stores = []
    for g, (copies, slots) in enumerate(loads):
        for copy in copies:
            copy.wait()
        found = [blocks[g, i] for i in range(QUAD)]
        for slot in slots:
            scales = quad_scales(coded, slot)
            for i in range(QUAD):
                found[i] += quad_code(coded, slot, i) * scales[i : i + 1]
        put_quad(results, g, found)
        stores.append(pltpu.make_async_copy(results.at[g], out.at[g], out_sems.at[g]))
        stores[-1].start()
    for copy in stores:
        copy.wait()


def combine(product, place, offset, firsts, *terms):
    side, width = product.shape[2:]
    tall, quads = QUAD * side + META, len(firsts)
    room = max(1, len(terms) * quads)
    hbm = pl.BlockSpec(memory_space=pl.ANY)
    return pl.pallas_call(
        functools.partial(combine_kernel, offset, firsts, [mode for _, mode in terms]),
        out_shape=jax.ShapeDtypeStruct((quads, tall, width), jnp.int16),
        in_specs=[pl.BlockSpec(memory_space=pltpu.SMEM)] + [hbm] * (1 + len(terms)),
        out_specs=hbm,
        scratch_shapes=[
            pltpu.VMEM((quads, QUAD, side, width), jnp.float32),
            pltpu.VMEM((room, tall, width), jnp.int16),
            pltpu.VMEM((quads, tall, width), jnp.int16),
            pltpu.SemaphoreType.DMA((quads,)),
            pltpu.SemaphoreType.DMA((room,)),
            pltpu.SemaphoreType.DMA((quads,)),
        ],
        compiler_params=pltpu.CompilerParams(vmem_limit_bytes=VMEM),
        cost_estimate=cost(8 << 20),
    )(place, product, *[array for array, _ in terms])


def row_sums(product):
    half = lax.axis_size("blk") // 2
    me = lax.axis_index("blk")
    place = jnp.stack([me // 2, me % 2]).astype(jnp.int32)
    product = product.reshape((half, product.shape[0] // half) + product.shape[1:])
    a = up(combine(product, place, 4, (0,)))
    b = down(combine(product, place, -4, (1,)))
    a = up(combine(product, place, 3, (0, 1), (a, 0)))
    b = down(combine(product, place, -3, (0, 1), (b, 1)))
    for step in (2, 1):
        a = up(combine(product, place, step, (0, 1), (a, "whole")))
        b = down(combine(product, place, -step, (0, 1), (b, "whole")))
    terms = ((a, "whole"), (b, "whole"))
    other = y_swap(combine(product, place, 0, ("other",), *terms))
    return combine(product, place, 0, ("mine",), *terms, (other, "single"))


def contrib_kernel(moves, arrays, base, owned, columns, *refs):
    owners, rank, cols, weights, values = refs[:5]
    pieces = refs[5 : 5 + arrays]
    out, slab, results, slab_sems, out_sems = refs[-5:]
    arrive = start_moves(moves, pieces, slab, slab_sems)
    firsts = [owners[base + k] * owned for k in range(slab.shape[0])]
    for copy in arrive:
        copy.wait()
    stores = []
    for k, first in enumerate(firsts):
        found = []
        scales = quad_scales(slab, k)
        for i in range(owned):
            code = quad_code(slab, k, i)
            high = code.astype(jnp.bfloat16)
            low = (code - high.astype(jnp.float32)).astype(jnp.bfloat16)
            both = jnp.concatenate([high, low], axis=1)
            product = lax.dot_general(
                values[first + i],
                both,
                (((0,), (0,)), ((), ())),
                preferred_element_type=jnp.float32,
            )
            width = high.shape[1]
            weight = scales[i : i + 1] * weights[first + i]
            found.append((product[:, :width] + product[:, width:]) * weight)
        extras = [lax.rem(cols[first + i], columns) for i in range(owned)]
        put_coded(results, k * owned, found, extras)
        for i in range(owned):
            slot = k * owned + i
            stores.append(
                pltpu.make_async_copy(
                    results.at[slot], out.at[rank[first + i]], out_sems.at[slot]
                )
            )
            stores[-1].start()
    for copy in stores:
        copy.wait()


def contribs(values, rank, cols, weights, shard, early, columns):
    blocks, side = values.shape[:2]
    owned = blocks // lax.axis_size("blk")
    owners = owner_table()

    def run(result, stage, base, shards):
        arrays, moves = stage_pieces(shards, stage, 1)
        quad, width = arrays[0].shape[1:]
        tall = side + META
        count = len(stage) * owned
        smem, hbm = pl.BlockSpec(memory_space=pltpu.SMEM), pl.BlockSpec(memory_space=pl.ANY)
        kept = pl.BlockSpec(memory_space=pltpu.VMEM)
        operands = [owners, rank, cols, weights, values, *arrays]
        aliases = {}
        if result is not None:
            aliases = {len(operands): 0}
            operands.append(result)
        return pl.pallas_call(
            functools.partial(contrib_kernel, moves, len(arrays), base, owned, columns),
            out_shape=jax.ShapeDtypeStruct((blocks, tall, width), jnp.int16),
            in_specs=[smem] * 4 + [kept] + [hbm] * (len(operands) - 5),
            out_specs=hbm,
            scratch_shapes=[
                pltpu.VMEM((len(stage), quad, width), jnp.int16),
                pltpu.VMEM((count, tall, width), jnp.int16),
                pltpu.SemaphoreType.DMA((len(moves),)),
                pltpu.SemaphoreType.DMA((count,)),
            ],
            input_output_aliases=aliases,
            compiler_params=pltpu.CompilerParams(vmem_limit_bytes=VMEM),
            cost_estimate=cost(count << 20),
        )(*operands)

    return gather_run(shard, early, run)


def three_parts(x):
    high = x.astype(jnp.bfloat16)
    rest = x - high.astype(jnp.float32)
    middle = rest.astype(jnp.bfloat16)
    return high, middle, (rest - middle.astype(jnp.float32)).astype(jnp.bfloat16)


def dot_down(a, b):
    return lax.dot_general(a, b, (((0,), (0,)), ((), ())), preferred_element_type=jnp.float32)


def column_kernel(slots, in_ref, out_ref, gram_ref):
    step = pl.program_id(0)
    count = in_ref.shape[0]

    @pl.when(step == 0)
    def _():
        out_ref[...] = jnp.zeros_like(out_ref)

    for i in range(count):
        slot = slots[step * count + i]
        out_ref[slot] += decoded(in_ref, i)

    @pl.when(step == pl.num_programs(0) - 1)
    def _():
        width = gram_ref.shape[0]
        main = jnp.zeros((2 * width, 2 * width), jnp.float32)
        rest = jnp.zeros((width, width), jnp.float32)
        for c in range(out_ref.shape[0]):
            high, middle, low = three_parts(out_ref[c])
            pair = jnp.concatenate([high, middle], axis=1)
            main += dot_down(pair, pair)
            rest += dot_down(high, low)
        rest += main[:width, width:]
        gram_ref[...] = main[:width, :width] + (rest + rest.T + main[width:, width:])


def column_sums(parts, slots, columns):
    blocks, tall, width = parts.shape
    batch = 16
    return pl.pallas_call(
        column_kernel,
        out_shape=(
            jax.ShapeDtypeStruct((columns, tall - META, width), jnp.float32),
            jax.ShapeDtypeStruct((width, width), jnp.float32),
        ),
        grid_spec=pltpu.PrefetchScalarGridSpec(
            num_scalar_prefetch=1,
            grid=(blocks // batch,),
            in_specs=[pl.BlockSpec((batch, tall, width), lambda s, *_: (s, 0, 0))],
            out_specs=(
                pl.BlockSpec((columns, tall - META, width), lambda s, *_: (0, 0, 0)),
                pl.BlockSpec((width, width), lambda s, *_: (0, 0)),
            ),
        ),
        compiler_params=pltpu.CompilerParams(vmem_limit_bytes=VMEM),
    )(slots, parts)


def gram_total(gram):
    size = gram.shape[0]
    parts = lax.axis_size("row")
    some = lax.all_to_all(gram, "row", 0, 0, tiled=True)
    some = jnp.sum(some.reshape(parts, size // parts, size), axis=0)
    count = lax.axis_size("blk")
    some = jnp.broadcast_to(some[None], (count,) + some.shape)
    some = jnp.sum(lax.all_to_all(some, "blk", 0, 0, tiled=True), axis=0)
    some = jnp.broadcast_to(some[None], (parts,) + some.shape)
    return lax.all_to_all(some, "row", 0, 0, tiled=True).reshape(size, size)


PANEL = 32
GROUP = 4


def inverse_root(x):
    y = lax.rsqrt(x)
    return y * (1.5 - 0.5 * x * y * y)


def eliminate(panel, other, first, down):
    size = panel.shape[1]
    for q in range(0, PANEL, GROUP):
        j = first + q
        columns = [jnp.broadcast_to(panel[:, j + b : j + b + 1], panel.shape) for b in range(GROUP)]
        rows = [panel[q + a : q + a + 1] for a in range(GROUP)]
        others = [other[q + a : q + a + 1] for a in range(GROUP)]
        lower, inverse = {}, []
        for b in range(GROUP):
            for c in range(b, GROUP):
                entry = columns[c][q + b : q + b + 1]
                for k in range(b):
                    entry = entry - lower[b, k] * lower[c, k]
                if c == b:
                    inverse.append(inverse_root(entry))
                else:
                    lower[c, b] = entry * inverse[b]
        for b in range(GROUP):
            for k in range(b):
                rows[b] = rows[b] - lower[b, k] * rows[k]
                others[b] = others[b] - lower[b, k] * others[k]
                columns[b] = columns[b] - lower[b, k] * columns[k]
            rows[b] = rows[b] * inverse[b]
            others[b] = others[b] * inverse[b]
            columns[b] = columns[b] * inverse[b]
        if q + GROUP < PANEL:
            below = down >= q + GROUP
            change = sum(c * r for c, r in zip(columns, rows))
            panel = jnp.where(below, panel - change, panel)
            change = sum(c * r for c, r in zip(columns, others))
            other = jnp.where(below, other - change, other)
        for b in range(GROUP):
            panel = jnp.where(down == q + b, rows[b], panel)
            other = jnp.where(down == q + b, others[b], other)
    across = lax.broadcasted_iota(jnp.int32, (PANEL, size), 1)
    return jnp.where(across >= down + first, panel, 0.0), other


def factor_kernel(gram_ref, sums_ref, basis_ref, upper_ref, g_ref, m_ref):
    size = gram_ref.shape[0]
    down = lax.broadcasted_iota(jnp.int32, (PANEL, size), 0)
    g_ref[...] = gram_ref[...] * (1.0 / (NCB * BS))
    m_ref[...] = (
        lax.broadcasted_iota(jnp.int32, (size, size), 0)
        == lax.broadcasted_iota(jnp.int32, (size, size), 1)
    ).astype(jnp.float32)
    for first in range(0, size, PANEL):
        here, after = pl.ds(first, PANEL), pl.ds(first + PANEL, size - first - PANEL)
        panel, other = eliminate(g_ref[here, :], m_ref[here, :], first, down)
        upper_ref[here, :] = panel
        m_ref[here, :] = other
        if first + PANEL < size:
            high, middle, low = three_parts(panel)
            left = jnp.concatenate([high, middle, high, middle, high, low], axis=0)
            high, middle, low = three_parts(jnp.concatenate([panel, other], axis=1))
            right = jnp.concatenate([high, high, middle, middle, low, high], axis=0)
            update = dot_down(left, right)[first + PANEL :]
            g_ref[after, :] -= update[:, :size]
            m_ref[after, :] -= update[:, size:]
    high, middle, low = three_parts(m_ref[...].T)
    main = jnp.concatenate([jnp.concatenate([high, middle], axis=1)] * 2, axis=0)
    rest = jnp.concatenate([low, high], axis=0)
    for c in range(sums_ref.shape[0]):
        high, middle, low = three_parts(sums_ref[c])
        first = jnp.dot(
            jnp.concatenate([high, middle], axis=1), main, preferred_element_type=jnp.float32
        )
        second = jnp.dot(
            jnp.concatenate([high, low], axis=1), rest, preferred_element_type=jnp.float32
        )
        basis_ref[c] = first[:, :size] + (first[:, size:] + second)


def factor(gram, sums):
    return pl.pallas_call(
        factor_kernel,
        out_shape=(
            jax.ShapeDtypeStruct(sums.shape, jnp.float32),
            jax.ShapeDtypeStruct(gram.shape, jnp.float32),
        ),
        in_specs=[pl.BlockSpec(memory_space=pltpu.VMEM)] * 2,
        out_specs=(pl.BlockSpec(memory_space=pltpu.VMEM),) * 2,
        scratch_shapes=[pltpu.VMEM(gram.shape, jnp.float32)] * 2,
        compiler_params=pltpu.CompilerParams(vmem_limit_bytes=VMEM),
    )(gram, sums)


def local(values, scales, pattern, omega):
    blocks = pattern.size
    columns, side, width = omega.shape
    parts = lax.axis_size("blk")
    values = values.reshape(blocks, side, side)
    cols = pattern.reshape(-1) - lax.axis_index("row") * columns * parts
    weights = scales.astype(jnp.float32).reshape(-1)
    count = lax.iota(jnp.int32, blocks)
    key = cols * blocks + count
    rank = jnp.sum((key[None, :] < key[:, None]).astype(jnp.int32), axis=1)
    order = jnp.sum(jnp.where(rank[None, :] == count[:, None], count[None, :], 0), axis=1)

    product = products(values, order, cols, weights, omega, columns - columns // 4, columns)
    rowvec = row_sums(product)
    coded = contribs(values, rank, cols, weights, rowvec, rowvec.shape[0], columns)
    coded = lax.all_to_all(coded, "blk", 0, 0, tiled=True)
    sums, gram = column_sums(coded, coded[:, side + 2, 0].astype(jnp.int32), columns)
    return factor(gram_total(gram), sums)


def solution(mesh):
    return jax.shard_map(
        local,
        mesh=mesh,
        in_specs=(
            P("row", "blk", None, None),
            P("row", "blk"),
            P("row", "blk"),
            P(("row", "blk"), None, None),
        ),
        out_specs=(P(("row", "blk"), None, None), P()),
        check_vma=False,
    )
```
